256 devices in a mesh: dp: 4 (over x), seq: 16 (over z, core), mp: 4 (over y).
Axes of the slice: x: 4, y: 4, z: 8, core: 2. Of those that a mesh axis runs over, the one named last changes fastest.
Arguments:
- patches: bfloat16 [16384, 3072], P(('dp', 'seq'), 'mp'), may hold values from -20 to 20
- image_of: int32 [16384], P(('dp', 'seq')), may hold values from 0 to 31, as said below
- prompt_of: int32 [4, 32], P('dp', 'seq'), may hold values from 0 to 15
- text_len: int32 [4, 16], P('dp'), may hold values from 1 to 256, as said below
- text_kv: bfloat16 [64, 256, 2, 1536], P('dp', 'seq', None, 'mp'), may hold values from -70 to 70
- w_qkv: bfloat16 [3072, 3, 1536], P(None, None, 'mp'), may hold values from -0.109375 to 0.109375
- w_out: bfloat16 [1536, 3072], P('mp'), may hold values from -0.15625 to 0.15625
- pre_gain: float32 [3072], replicated, may hold values from 0.1 to 1.9
- pre_bias: float32 [3072], replicated, may hold values from -3 to 3
- post_gain: float32 [3072], replicated, may hold values from 0.1 to 1.9
- post_bias: float32 [3072], replicated, may hold values from -3 to 3
Outputs:
- block_out: bfloat16 [16384, 3072], P(('dp', 'seq'), 'mp')
The draws below stay inside these ranges and needn't reach their ends.
Inputs may be any that keep to these rules, and one draw needn't show every extreme that they name: `image_of`: the rows of one device name each image at most 16 times; in every data-parallel group one image is named exactly 16 times by the rows of every device of that group. `text_len`: in every data-parallel group some prompt has all 256 tokens live.
All inputs are finite; a program needn't handle non-finite values.
Results may differ from the reference program's by a relative error of at most 0.011.
Values may be sent and summed in bfloat16 or wider, within the bound.
A program may use at most 128 MiB of HBM per device.

```python
import math
import jax
import jax.numpy as jnp
from jax import lax

D = 3072
HEADS = 12
HD = 128
TXT = 256
TOK_DEV = 256
PROMPT_GRP = 16
NIMG = 32
MOST = 16
TOKENS = 16384
PROMPTS = 64
N_DP = 4
N_SEQ = 16


def draw_patches(key, part):
    key_col, key_row, key_main = jax.random.split(key, 3)
    column_ids = jnp.arange(D, dtype=jnp.float32)
    column_scale = 0.05 * 3.0 ** (column_ids / D) * 10.0 ** jax.random.uniform(key_col, (D,), jnp.float32, 0.0, 1.0)
    row_scale = 0.3 * 10.0 ** jax.random.uniform(key_row, (TOKENS, 1), jnp.float32, 0.0, 1.0)
    samples = jax.random.truncated_normal(key_main, -4.0, 4.0, (TOKENS, D), jnp.float32)
    return jnp.clip(samples * column_scale * row_scale, -20.0, 20.0).astype(jnp.bfloat16)


def draw_image_of(key, part):
    slot_count = NIMG * MOST
    key_size, key_pick, key_score, key_order = jax.random.split(key, 4)
    image_sizes = jax.random.randint(key_size, (N_DP, NIMG), MOST // 2, MOST + 1)
    chosen = jax.random.randint(key_pick, (N_DP,), 0, NIMG)
    marked = jnp.arange(NIMG, dtype=jnp.int32)[None, :] == chosen[:, None]
    image_sizes = jnp.where(marked, MOST, image_sizes)
    slot_ids = jnp.arange(slot_count, dtype=jnp.int32)
    image_ids = slot_ids // MOST
    slot_depth = slot_ids % MOST
    eligible = slot_depth[None, None, :] < image_sizes[:, image_ids][:, None, :]
    favored = marked[:, image_ids][:, None, :]
    priority = jax.random.randint(key_score, (N_DP, N_SEQ, slot_count), 0, 2 ** 16) * slot_count + slot_ids[None, None, :]
    priority = jnp.where(eligible, priority, priority + 2 ** 30)
    priority = jnp.where(favored, slot_ids[None, None, :] - slot_count, priority)
    selected = jnp.argsort(priority, axis=-1)[..., :TOK_DEV]
    image_pick = selected // MOST
    shuffle = jax.random.randint(key_order, (N_DP, N_SEQ, TOK_DEV), 0, 2 ** 16) * TOK_DEV + jnp.arange(TOK_DEV, dtype=jnp.int32)[None, None, :]
    permuted = jnp.argsort(shuffle, axis=-1)
    image_pick = jnp.take_along_axis(image_pick, permuted, axis=-1)
    return image_pick.reshape(TOKENS).astype(jnp.int32)


def draw_text_len(key, part):
    key_len, key_pick = jax.random.split(key)
    lengths = jax.random.randint(key_len, (N_DP, PROMPT_GRP), 1, TXT + 1)
    picked = jax.random.randint(key_pick, (N_DP, 1), 0, PROMPT_GRP)
    lengths = jnp.where(jnp.arange(PROMPT_GRP, dtype=jnp.int32)[None, :] == picked, TXT, lengths)
    return lengths.astype(jnp.int32)


def draw_text_kv(key, part):
    full_shape = (PROMPTS, TXT, 2, HEADS * HD)
    key_main = jax.random.fold_in(key, 0)
    samples = jax.random.truncated_normal(key_main, -4.0, 4.0, full_shape, jnp.float32)
    return samples.astype(jnp.bfloat16)


def place_ends(entries, rng, smallest, top_value):
    place = [jax.random.randint(jax.random.fold_in(rng, axis), (), 0, length) for axis, length in enumerate(entries.shape)]
    widest = entries.shape.index(max(entries.shape))
    neighbour = place[:widest] + [(place[widest] + 1) % entries.shape[widest]] + place[widest + 1:]
    return entries.at[tuple(place)].set(smallest).at[tuple(neighbour)].set(top_value)


def shard_levels(rng, dims, shards, least, top_value):
    level, own = 1.0, jax.random.fold_in(rng, 6)
    for axis_at, blocks in shards:
        heights = jnp.exp(jax.random.uniform(jax.random.fold_in(own, axis_at), (blocks,), jnp.float32, least / len(shards), top_value / len(shards)))
        level = level * jnp.repeat(heights, dims[axis_at] // blocks).reshape([-1 if axis == axis_at else 1 for axis in range(len(dims))])
    return level


def scatter_about(stream_key, shape, width, most, cuts=(), kind=jnp.bfloat16):
    drawn = width * jax.random.normal(stream_key, shape, jnp.float32)
    if cuts:
        drawn = drawn * shard_levels(stream_key, shape, cuts, -0.22, 0.18)
    return jnp.clip(drawn, -most, most).astype(kind)


def setup_inputs(seed: int = 0) -> dict:
    key_list = jax.random.split(jax.random.key(seed), 12)
    patches = draw_patches(jax.random.fold_in(key_list[11], 71), 0)
    image_of = draw_image_of(jax.random.fold_in(key_list[11], 71), 0)
    prompt_of = place_ends(jax.random.randint(key_list[2], (N_DP, NIMG), 0, PROMPT_GRP), jax.random.fold_in(key_list[2], 1), 0, PROMPT_GRP - 1).astype(jnp.int32)
    text_len = draw_text_len(jax.random.fold_in(key_list[11], 71), 0)
    text_kv = draw_text_kv(jax.random.fold_in(key_list[11], 71), 0)
    w_qkv = scatter_about(key_list[5], (D, 3, HEADS * HD), D ** -0.5, 0.109375, ((2, 4),))
    w_out = scatter_about(key_list[6], (HEADS * HD, D), (HEADS * HD) ** -0.5, 0.15625, ((0, 4),))
    pre_gain = jnp.clip(1.0 + 0.18 * jax.random.normal(key_list[7], (D,), jnp.float32), 0.1, 1.9)
    pre_bias = scatter_about(key_list[8], (D,), 0.5, 3.0, (), jnp.float32)
    post_gain = jnp.clip(1.0 + 0.18 * jax.random.normal(key_list[9], (D,), jnp.float32), 0.1, 1.9)
    post_bias = scatter_about(key_list[10], (D,), 0.5, 3.0, (), jnp.float32)
    return dict(patches=patches, image_of=image_of, prompt_of=prompt_of, text_len=text_len, text_kv=text_kv, w_qkv=w_qkv, w_out=w_out, pre_gain=pre_gain, pre_bias=pre_bias, post_gain=post_gain, post_bias=post_bias)


epsilon = 1e-05

def layer_norm(values_in, gain_vec, bias_vec):
    average = lax.optimization_barrier(jnp.mean(values_in, axis=-1, keepdims=True))
    centered = values_in - average
    spread = lax.optimization_barrier(jnp.mean(centered * centered, axis=-1, keepdims=True))
    return centered * lax.rsqrt(spread + epsilon) * gain_vec + bias_vec

def reference(patches, image_of, prompt_of, text_len, text_kv, w_qkv, w_out, pre_gain, pre_bias, post_gain, post_bias):
    group_rows = TOK_DEV * N_SEQ
    head_cols = HEADS * HD
    softmax_scale = 1.0 / math.sqrt(HD)
    block_rows = 512 if group_rows % 512 == 0 else group_rows
    normed = layer_norm(patches.astype(jnp.float32), pre_gain, pre_bias).astype(jnp.bfloat16)
    projections = jnp.dot(normed, w_qkv.reshape(D, 3 * head_cols), preferred_element_type=jnp.float32).astype(jnp.bfloat16)
    projections = lax.optimization_barrier(projections).astype(jnp.float32)
    token_prompt = jnp.repeat(jnp.arange(PROMPT_GRP, dtype=jnp.int32), TXT)
    token_place = jnp.tile(jnp.arange(TXT, dtype=jnp.int32), PROMPT_GRP)
    pieces = []
    for group_index in range(N_DP):
        first_row = group_index * group_rows
        images = image_of[first_row:first_row + group_rows].astype(jnp.int32)
        group_proj = projections[first_row:first_row + group_rows]
        queries = group_proj[:, :head_cols].reshape(group_rows, HEADS, HD)
        image_key_rows = group_proj[:, head_cols:2 * head_cols].reshape(group_rows, HEADS, HD)
        vals_img = group_proj[:, 2 * head_cols:].reshape(group_rows, HEADS, HD)
        text_group = text_kv[group_index * PROMPT_GRP:(group_index + 1) * PROMPT_GRP].astype(jnp.float32)
        keys_txt = text_group[:, :, 0].reshape(PROMPT_GRP * TXT, HEADS, HD)
        vals_txt = text_group[:, :, 1].reshape(PROMPT_GRP * TXT, HEADS, HD)
        lengths = text_len[group_index].astype(jnp.int32)
        token_live = token_place < lengths[token_prompt]
        row_prompt = prompt_of[group_index].astype(jnp.int32)[images]
        joint_value_rows = jnp.concatenate([vals_img, vals_txt], axis=0)

        def one_block(offset):
            query_tile_rows = lax.dynamic_slice_in_dim(queries, offset, block_rows, 0)
            image_block = lax.dynamic_slice_in_dim(images, offset, block_rows, 0)
            prompt_block = lax.dynamic_slice_in_dim(row_prompt, offset, block_rows, 0)
            image_score_matrix = jnp.einsum('pgr,ygr->gpy', query_tile_rows, image_key_rows) * softmax_scale
            same_image = image_block[:, None] == images[None, :]
            image_score_matrix = jnp.where(same_image[None], image_score_matrix, -jnp.inf)
            scores_txt = jnp.einsum('bhd,thd->hbt', query_tile_rows, keys_txt) * softmax_scale
            same_prompt = (prompt_block[:, None] == token_prompt[None, :]) & token_live[None, :]
            scores_txt = jnp.where(same_prompt[None], scores_txt, -jnp.inf)
            scores = jnp.concatenate([image_score_matrix, scores_txt], axis=-1)
            highest = lax.optimization_barrier(jnp.max(scores, axis=-1, keepdims=True))
            exponent = jnp.exp(scores - highest)
            attention_probs = (exponent / lax.optimization_barrier(jnp.sum(exponent, axis=-1, keepdims=True))).astype(jnp.bfloat16)
            attention_probs = lax.optimization_barrier(attention_probs).astype(jnp.float32)
            mixed_output = jnp.einsum('eua,aek->uek', attention_probs, joint_value_rows)
            return mixed_output.astype(jnp.bfloat16)
        offsets = jnp.arange(0, group_rows, block_rows, dtype=jnp.int32)
        attended_group = lax.map(one_block, offsets).reshape(group_rows, head_cols)
        pieces.append(attended_group)
    attended = jnp.concatenate(pieces, axis=0)
    projected = jnp.dot(attended, w_out, preferred_element_type=jnp.float32)
    block_out = patches.astype(jnp.float32) + layer_norm(projected, post_gain, post_bias)
    return block_out.astype(jnp.bfloat16)
```

```python
import math

import jax
import jax.numpy as jnp
from jax import lax
from jax.experimental import pallas as pl
from jax.experimental.pallas import tpu as pltpu
from jax.sharding import PartitionSpec as P

HD = 128
EPS = 1e-05
MESH = pl.DeviceIdType.MESH
NEG = -1e30

f32 = jnp.float32
bf16 = jnp.bfloat16
i32 = jnp.int32


def iota(shape, dim):
    return lax.broadcasted_iota(i32, shape, dim)


def fused(
    x_ref, img_ref, prm_ref, len_ref, text_ref, w_ref, wo_ref, pg_ref, pb_ref, qg_ref, qb_ref,
    o_ref,
    xs, xg, xn, wv, wc, qkv, ts, tr, ret, ag, ms, mr, mrs, st, sr, kb,
    zss, zrs, tss, trs, mss, mrsem, yss, yrs, rss, rrs, y2s, y2r, wss, wrs, bss, brs, sss, srs, lsem,
):
    s = lax.axis_index("seq")
    m = lax.axis_index("mp")
    NS, MP = xg.shape[1], xg.shape[0]
    rows = x_ref.shape[0]
    cols = x_ref.shape[1]
    slots = xs.shape[2] * xs.shape[1] * NS
    depth = xs.shape[2]
    nimg = 2 * NS
    heads = qkv.shape[3] // HD
    right = lax.rem(m + 1, MP)
    left = lax.rem(m + MP - 1, MP)
    far = lax.rem(m + 2, MP)
    core = lax.rem(s, 2)
    sib = s + 1 - 2 * core

    def seq_at(k):
        return lax.rem(s + k, NS)

    def step_k(t):
        half = (t + 1) // 2
        return jnp.where(lax.rem(t, 2) == 1, half, lax.rem(NS - half, NS))

    bar = pltpu.get_barrier_semaphore()

    @pl.loop(1, NS)
    def _(k):
        pl.semaphore_signal(bar, inc=1, device_id={"seq": seq_at(k)}, device_id_type=MESH)

    for d in (right, left, far):
        pl.semaphore_signal(bar, inc=1, device_id={"mp": d}, device_id_type=MESH)

    wcp = pltpu.make_async_copy(w_ref, wv, lsem.at[0])
    wcp.start()
    ocp = pltpu.make_async_copy(wo_ref.at[:, pl.ds(pl.multiple_of(m * cols, 128), cols)], wc.at[m], lsem.at[1])
    ocp.start()

    img = img_ref[...]
    onehot = (jnp.broadcast_to(img, (nimg, rows)) == iota((nimg, rows), 0)).astype(f32)
    upto = (iota((rows, rows), 0) <= iota((rows, rows), 1)).astype(bf16)
    cum = jnp.dot(onehot.astype(bf16), upto, preferred_element_type=f32)
    rank = jnp.sum(cum * onehot, axis=0, keepdims=True) - 1.0
    pos = img.astype(f32) * depth + rank
    counts = jnp.sum(onehot, axis=1, keepdims=True)
    crow = jnp.sum(
        jnp.where(iota((nimg, 128), 0) == iota((nimg, 128), 1), jnp.broadcast_to(counts, (nimg, 128)), 0.0),
        axis=0, keepdims=True,
    ).astype(i32)
    lane = iota((1, 128), 1)
    crow = jnp.where(lane == nimg, prm_ref[0, 0], jnp.where(lane == nimg + 1, prm_ref[0, 1], crow))
    ms[...] = crow
    mr[s] = crow
    place = (jnp.broadcast_to(pos, (slots, rows)) == iota((slots, rows), 0).astype(f32)).astype(bf16)
    spread = jnp.dot(place, x_ref[...], preferred_element_type=f32).astype(bf16)
    xs[...] = spread.reshape(xs.shape)
    xg[m, s] = xs[s]

    pl.semaphore_wait(bar, NS - 1 + 3)

    def zcopy(d, c):
        return pltpu.make_async_remote_copy(
            src_ref=xs.at[d], dst_ref=xg.at[m, c], send_sem=zss.at[d], recv_sem=zrs.at[c],
            device_id={"seq": d}, device_id_type=MESH)

    def tcopy(d, c):
        return pltpu.make_async_remote_copy(
            src_ref=ts.at[d], dst_ref=tr.at[c], send_sem=tss.at[d], recv_sem=trs.at[c],
            device_id={"seq": d}, device_id_type=MESH)

    def mcopy(d, c):
        return pltpu.make_async_remote_copy(
            src_ref=ms, dst_ref=mr.at[c], send_sem=mss.at[d], recv_sem=mrsem.at[c],
            device_id={"seq": d}, device_id_type=MESH)

    def rcopy(d, c):
        return pltpu.make_async_remote_copy(
            src_ref=ret.at[d], dst_ref=ag.at[m, c], send_sem=rss.at[d], recv_sem=rrs.at[c],
            device_id={"seq": d}, device_id_type=MESH)

    def relay(buf, ssem, rsem):
        def one(y, c, part, lane_of, to):
            ref = buf.at[y, c] if part is None else buf.at[y, c, part]
            return pltpu.make_async_remote_copy(
                src_ref=ref, dst_ref=ref, send_sem=ssem.at[lane_of, c], recv_sem=rsem.at[lane_of, c],
                device_id={"mp": to}, device_id_type=MESH)

        first = lambda c: (one(m, c, None, 0, right), one(m, c, None, 1, left))
        second = lambda c: (one(left, c, 0, 2, right), one(right, c, 1, 3, left))
        got_left = lambda c: one(left, c, None, 0, right)
        got_right = lambda c: one(right, c, None, 1, left)
        got_far0 = lambda c: one(far, c, 0, 2, right)
        got_far1 = lambda c: one(far, c, 1, 3, left)

        def open_(c):
            a, b = first(c)
            a.start()
            b.start()

        def pass_on(c):
            a, b = second(c)
            got_left(c).wait_recv()
            a.start()
            got_right(c).wait_recv()
            b.start()

        def arrived(c):
            got_far0(c).wait_recv()
            got_far1(c).wait_recv()

        def drain(c):
            for cp in first(c) + second(c):
                cp.wait_send()

        return open_, pass_on, arrived, drain

    @pl.loop(1, NS)
    def _(k):
        mcopy(seq_at(k), s).start()

    @pl.loop(1, NS)
    def _(t):
        zcopy(seq_at(step_k(t)), s).start()

    @pl.loop(1, NS)
    def _(k):
        c = seq_at(k)
        mcopy(c, c).wait()

    scp = pltpu.make_async_copy(mr, mrs, lsem.at[2])
    scp.start()
    scp.wait()

    @pl.loop(0, NS)
    def _(d):
        for i in range(2):
            ts[d, i] = text_ref[mrs[d, 0, nimg + i]]

    tr[s] = ts[s]

    open1, pass1, arrived1, drain1 = relay(xg, yss, yrs)
    LAG1, LAG2 = 2, 4

    def norm_chunk(c):
        parts = [xg[y, c].astype(f32) for y in range(MP)]
        total = sum(jnp.sum(p, axis=-1, keepdims=True) for p in parts)
        mean = total / (MP * cols)
        parts = [p - mean for p in parts]
        var = sum(jnp.sum(p * p, axis=-1, keepdims=True) for p in parts) / (MP * cols)
        inv = lax.rsqrt(var + EPS)
        for y in range(MP):
            g = pg_ref[:, y * cols:(y + 1) * cols].reshape(1, 1, cols)
            b = pb_ref[:, y * cols:(y + 1) * cols].reshape(1, 1, cols)
            n = (parts[y] * inv * g + b).astype(bf16)
            for i in range(2):
                xn[i, c, :, y * cols:(y + 1) * cols] = n[i]

    @pl.loop(0, NS + LAG2)
    def _(t):
        @pl.when(t < NS)
        def _():
            k = step_k(t)
            c = lax.rem(s + NS - k, NS)
            d = seq_at(k)

            @pl.when(t > 0)
            def _():
                zcopy(c, c).wait_recv()

            open1(c)

            @pl.when(t > 0)
            def _():
                zcopy(d, s).wait_send()
                tcopy(d, s).start()

        @pl.when((t >= LAG1) & (t < NS + LAG1))
        def _():
            pass1(lax.rem(s + NS - step_k(t - LAG1), NS))

        @pl.when(t >= LAG2)
        def _():
            c = lax.rem(s + NS - step_k(t - LAG2), NS)
            arrived1(c)
            norm_chunk(c)

    hrows = wc.shape[1] // 2
    mine = pl.ds(pl.multiple_of(core * hrows, 16), hrows)

    def wcopy(y, k):
        return pltpu.make_async_remote_copy(
            src_ref=wo_ref.at[mine, pl.ds(pl.multiple_of(y * cols, 128), cols)], dst_ref=wc.at[m, mine],
            send_sem=wss.at[k], recv_sem=wrs.at[k], device_id={"mp": y}, device_id_type=MESH)

    def wgot(y, k):
        return pltpu.make_async_remote_copy(
            src_ref=wo_ref.at[mine, pl.ds(pl.multiple_of(y * cols, 128), cols)], dst_ref=wc.at[y, mine],
            send_sem=wss.at[k], recv_sem=wrs.at[k], device_id={"mp": y}, device_id_type=MESH)

    other = pl.ds(pl.multiple_of((1 - core) * hrows, 16), hrows)

    def bcopy(y, k, part):
        return pltpu.make_async_remote_copy(
            src_ref=wc.at[y, part], dst_ref=wc.at[y, part], send_sem=bss.at[k], recv_sem=brs.at[k],
            device_id={"seq": sib}, device_id_type=MESH)

    for k in (1, 3, 2):
        wcopy(lax.rem(m + k, MP), k).start()

    wcp.wait()
    normed = xn[...].reshape(slots, MP * cols)

    @pl.loop(0, 3)
    def _(j):
        r = jnp.dot(normed, wv[j], preferred_element_type=f32).astype(bf16)
        qkv[j] = r.reshape(qkv.shape[1:])

    span = NS * depth
    lanes = iota((1, span), 1)
    tlen = NS * depth
    for i in range(2):
        cnt = jnp.zeros((1, span), i32)
        for c in range(NS):
            cnt = jnp.where(lanes // depth == c, mrs[c, 0, 2 * s + i], cnt)
        kb[2 * i] = jnp.where(lax.rem(lanes, depth) < cnt, 0.0, NEG)
        n = len_ref[0, mrs[s, 0, nimg + i]]
        kb[2 * i + 1] = jnp.where(lanes < n, 0.0, NEG)

    @pl.loop(1, NS)
    def _(k):
        c = seq_at(k)
        tcopy(c, c).wait_recv()

    scale = 1.0 / math.sqrt(HD)
    nt = (((1,), (1,)), ((), ()))

    @pl.loop(0, 2)
    def _(i):
        bi = kb[2 * i]
        bt = kb[2 * i + 1]
        for h in range(heads):
            hs = slice(h * HD, (h + 1) * HD)
            q = qkv[0, i, :, hs]
            ki = qkv[1, i, :, hs]
            vi = qkv[2, i, :, hs]
            kt = tr[:, i, 0, :, hs].reshape(tlen, HD)
            vt = tr[:, i, 1, :, hs].reshape(tlen, HD)
            s1 = lax.dot_general(q, ki, nt, preferred_element_type=f32) * scale + bi
            s2 = lax.dot_general(q, kt, nt, preferred_element_type=f32) * scale + bt
            top = jnp.maximum(jnp.max(s1, axis=-1, keepdims=True), jnp.max(s2, axis=-1, keepdims=True))
            e1 = jnp.exp(s1 - top)
            e2 = jnp.exp(s2 - top)
            tot = jnp.sum(e1, axis=-1, keepdims=True) + jnp.sum(e2, axis=-1, keepdims=True)
            inv = 1.0 / tot
            p1 = (e1 * inv).astype(bf16)
            p2 = (e2 * inv).astype(bf16)
            o = jnp.dot(p1, vi, preferred_element_type=f32) + jnp.dot(p2, vt, preferred_element_type=f32)
            ret[:, i, :, hs] = o.astype(bf16).reshape(NS, depth, HD)

    @pl.loop(1, NS)
    def _(t):
        rcopy(seq_at(step_k(t)), s).start()

    ag[m, s] = ret[s]
    for k in (1, 3, 2):
        y = lax.rem(m + MP - k, MP)
        wgot(y, k).wait_recv()
        bcopy(y, k, mine).start()

    open2, pass2, arrived2, drain2 = relay(ag, y2s, y2r)

    @pl.loop(0, NS + LAG1)
    def _(t):
        @pl.when(t < NS)
        def _():
            k = step_k(t)
            c = lax.rem(s + NS - k, NS)

            @pl.when(t > 0)
            def _():
                rcopy(c, c).wait_recv()

            open2(c)

        @pl.when(t >= LAG1)
        def _():
            pass2(lax.rem(s + NS - step_k(t - LAG1), NS))

    @pl.loop(0, NS)
    def _(c):
        arrived2(c)

    ocp.wait()
    for k in (1, 3, 2):
        y = lax.rem(m + MP - k, MP)
        bcopy(y, k, other).wait_recv()

    eye = iota((rows, rows), 0) == iota((rows, rows), 1)

    def to_col(row):
        return jnp.sum(jnp.where(eye, jnp.broadcast_to(row, (rows, rows)), 0.0), axis=1, keepdims=True)

    def to_row(col):
        return jnp.sum(jnp.where(eye, jnp.broadcast_to(col, (rows, rows)), 0.0), axis=0, keepdims=True)

    pick = (jnp.broadcast_to(to_col(pos), (rows, slots)) == iota((rows, slots), 1).astype(f32)).astype(bf16)
    acc = jnp.zeros((rows, cols), f32)
    for y in range(MP):
        a = jnp.dot(pick, ag[y].reshape(slots, ag.shape[-1]), preferred_element_type=f32).astype(bf16)
        acc = acc + jnp.dot(a, wc[y], preferred_element_type=f32)

    mean = jnp.sum(acc, axis=1, keepdims=True) / cols
    dev = acc - mean
    m2 = jnp.sum(dev * dev, axis=1, keepdims=True)
    st[0:1, :] = to_row(mean)
    st[1:2, :] = to_row(m2)

    def scopy(k, to):
        return pltpu.make_async_remote_copy(
            src_ref=st, dst_ref=sr.at[k], send_sem=sss.at[k], recv_sem=srs.at[k],
            device_id={"mp": to}, device_id_type=MESH)

    for k in (1, 3, 2):
        scopy(k, lax.rem(m + k, MP)).start()

    @pl.loop(1, NS)
    def _(k):
        d = seq_at(k)
        tcopy(d, s).wait_send()
        rcopy(d, s).wait_send()

    @pl.loop(0, NS)
    def _(c):
        drain1(c)
        drain2(c)

    for k in (1, 3, 2):
        wcopy(lax.rem(m + k, MP), k).wait_send()
        bcopy(lax.rem(m + MP - k, MP), k, mine).wait_send()

    for k in (1, 3, 2):
        scopy(k, lax.rem(m + k, MP)).wait()

    means = [st[0:1, :]] + [sr[k, 0:1, :] for k in (1, 2, 3)]
    m2s = [st[1:2, :]] + [sr[k, 1:2, :] for k in (1, 2, 3)]
    avg = sum(means) / MP
    sq = sum(m2s) + cols * sum((u - avg) * (u - avg) for u in means)
    rstd = lax.rsqrt(sq / (MP * cols) + EPS)
    avg_c = to_col(avg)
    rstd_c = to_col(rstd)
    own = pl.ds(pl.multiple_of(m * cols, 128), cols)
    n = (acc - avg_c) * rstd_c * qg_ref[:, own] + qb_ref[:, own]
    o_ref[...] = (x_ref[...].astype(f32) + n).astype(bf16)


def shards(
    patches, image_of, prompt_of, text_len, text_kv, w_qkv, w_out, pre_gain, pre_bias, post_gain, post_bias,
):
    NS = lax.axis_size("seq")
    MP = lax.axis_size("mp")
    rows, cols = patches.shape
    depth = rows // NS
    hc = w_out.shape[0]
    toks = text_kv.shape[1]
    text = jnp.transpose(text_kv, (0, 2, 1, 3))
    w = jnp.transpose(w_qkv, (1, 0, 2))
    full = w_qkv.shape[0]
    vm = pl.BlockSpec(memory_space=pltpu.VMEM)
    sm = pl.BlockSpec(memory_space=pltpu.SMEM)
    anys = pl.BlockSpec(memory_space=pl.ANY)
    dma = pltpu.SemaphoreType.DMA
    return pl.pallas_call(
        fused,
        out_shape=jax.ShapeDtypeStruct((rows, cols), bf16),
        in_specs=[vm, vm, sm, sm, vm, anys, anys, vm, vm, vm, vm],
        out_specs=vm,
        scratch_shapes=[
            pltpu.VMEM((NS, 2, depth, cols), bf16),
            pltpu.VMEM((MP, NS, 2, depth, cols), bf16),
            pltpu.VMEM((2, NS, depth, full), bf16),
            pltpu.VMEM((3, full, hc), bf16),
            pltpu.VMEM((MP, hc, cols), bf16),
            pltpu.VMEM((3, 2, NS * depth, hc), bf16),
            pltpu.VMEM((NS, 2, 2, toks, hc), bf16),
            pltpu.VMEM((NS, 2, 2, toks, hc), bf16),
            pltpu.VMEM((NS, 2, depth, hc), bf16),
            pltpu.VMEM((MP, NS, 2, depth, hc), bf16),
            pltpu.VMEM((1, 128), i32),
            pltpu.VMEM((NS, 1, 128), i32),
            pltpu.SMEM((NS, 1, 128), i32),
            pltpu.VMEM((8, rows), f32),
            pltpu.VMEM((MP, 8, rows), f32),
            pltpu.VMEM((4, 1, NS * depth), f32),
            dma((NS,)), dma((NS,)), dma((NS,)), dma((NS,)), dma((NS,)), dma((NS,)),
            dma((4, NS)), dma((4, NS)), dma((NS,)), dma((NS,)), dma((4, NS)), dma((4, NS)),
            dma((4,)), dma((4,)), dma((4,)), dma((4,)), dma((4,)), dma((4,)), dma((3,)),
        ],
        compiler_params=pltpu.CompilerParams(collective_id=0, has_side_effects=True, vmem_limit_bytes=50 << 20),
    )(
        patches, image_of.reshape(1, rows), prompt_of, text_len, text, w, w_out,
        pre_gain.reshape(1, -1), pre_bias.reshape(1, -1), post_gain.reshape(1, -1), post_bias.reshape(1, -1),
    )


def solution(mesh):
    placed = (
        P(("dp", "seq"), "mp"),
        P(("dp", "seq")),
        P("dp", "seq"),
        P("dp", None),
        P("dp", "seq", None, "mp"),
        P(None, None, "mp"),
        P("mp", None),
        P(),
        P(),
        P(),
        P(),
    )
    return jax.shard_map(
        shards, mesh=mesh, in_specs=placed, out_specs=P(("dp", "seq"), "mp"), check_vma=False
    )
```

```python
import math

import jax
import jax.numpy as jnp
from jax import lax
from jax.experimental import pallas as pl
from jax.experimental.pallas import tpu as pltpu
from jax.sharding import PartitionSpec as P

HD = 128
EPS = 1e-05
MESH = pl.DeviceIdType.MESH
NEG = -1e30

f32 = jnp.float32
bf16 = jnp.bfloat16
i32 = jnp.int32


def iota(shape, dim):
    return lax.broadcasted_iota(i32, shape, dim)


def fused(
    x_in, img_in, prm_ref, len_ref, text_ref, w_ref, wo_ref, pg_in, pb_in, qg_in, qb_in,
    o_ref,
    x_ref, img_ref, pg_ref, pb_ref, qg_ref, qb_ref, xs, xg, xn, wv, wc, qkv, ts, tr, ret, ag, ms, mr, mrs, st, sr, kb,
    zss, zrs, tss, trs, mss, mrsem, yss, yrs, rss, rrs, y2s, y2r, wss, wrs, bss, brs, sss, srs, lsem,
):
    s = lax.axis_index("seq")
    m = lax.axis_index("mp")
    NS, MP = xg.shape[1], xg.shape[0]
    rows = x_ref.shape[0]
    cols = x_ref.shape[1]
    slots = xs.shape[2] * xs.shape[1] * NS
    depth = xs.shape[2]
    nimg = 2 * NS
    heads = qkv.shape[3] // HD
    right = lax.rem(m + 1, MP)
    left = lax.rem(m + MP - 1, MP)
    far = lax.rem(m + 2, MP)
    core = lax.rem(s, 2)
    sib = s + 1 - 2 * core

    def seq_at(k):
        return lax.rem(s + k, NS)

    def step_k(t):
        half = (t + 1) // 2
        return jnp.where(lax.rem(t, 2) == 1, half, lax.rem(NS - half, NS))

    bar = pltpu.get_barrier_semaphore()

    @pl.loop(1, NS)
    def _(k):
        pl.semaphore_signal(bar, inc=1, device_id={"seq": seq_at(k)}, device_id_type=MESH)

    for d in (right, left, far):
        pl.semaphore_signal(bar, inc=1, device_id={"mp": d}, device_id_type=MESH)

    loads = []
    for n, (a, b) in enumerate(
        ((img_in, img_ref), (x_in, x_ref), (pg_in, pg_ref), (pb_in, pb_ref), (qg_in, qg_ref), (qb_in, qb_ref))
    ):
        loads.append(pltpu.make_async_copy(a, b, lsem.at[3 + n]))
        loads[-1].start()
    wcp = pltpu.make_async_copy(w_ref, wv, lsem.at[0])
    wcp.start()
    ocp = pltpu.make_async_copy(wo_ref.at[:, pl.ds(pl.multiple_of(m * cols, 128), cols)], wc.at[m], lsem.at[1])
    ocp.start()

    loads[0].wait()
    img = img_ref[...]
    onehot = (jnp.broadcast_to(img, (nimg, rows)) == iota((nimg, rows), 0)).astype(f32)
    upto = (iota((rows, rows), 0) <= iota((rows, rows), 1)).astype(bf16)
    cum = jnp.dot(onehot.astype(bf16), upto, preferred_element_type=f32)
    rank = jnp.sum(cum * onehot, axis=0, keepdims=True) - 1.0
    pos = img.astype(f32) * depth + rank
    counts = jnp.sum(onehot, axis=1, keepdims=True)
    crow = jnp.sum(
        jnp.where(iota((nimg, 128), 0) == iota((nimg, 128), 1), jnp.broadcast_to(counts, (nimg, 128)), 0.0),
        axis=0, keepdims=True,
    ).astype(i32)
    lane = iota((1, 128), 1)
    crow = jnp.where(lane == nimg, prm_ref[0, 0], jnp.where(lane == nimg + 1, prm_ref[0, 1], crow))
    ms[...] = crow
    mr[s] = crow
    place = (jnp.broadcast_to(pos, (slots, rows)) == iota((slots, rows), 0).astype(f32)).astype(bf16)
    loads[1].wait()
    spread = jnp.dot(place, x_ref[...], preferred_element_type=f32).astype(bf16)
    xs[...] = spread.reshape(xs.shape)
    xg[m, s] = xs[s]

    pl.semaphore_wait(bar, NS - 1 + MP - 1)

    def zcopy(d, c):
        return pltpu.make_async_remote_copy(
            src_ref=xs.at[d], dst_ref=xg.at[m, c], send_sem=zss.at[d], recv_sem=zrs.at[c],
            device_id={"seq": d}, device_id_type=MESH)

    def tcopy(i, d, c):
        return pltpu.make_async_remote_copy(
            src_ref=ts.at[i, d], dst_ref=tr.at[i, c], send_sem=tss.at[i, d], recv_sem=trs.at[i, c],
            device_id={"seq": d}, device_id_type=MESH)

    def mcopy(d, c):
        return pltpu.make_async_remote_copy(
            src_ref=ms, dst_ref=mr.at[c], send_sem=mss.at[d], recv_sem=mrsem.at[c],
            device_id={"seq": d}, device_id_type=MESH)

    def rcopy(i, d, c):
        return pltpu.make_async_remote_copy(
            src_ref=ret.at[i, d], dst_ref=ag.at[m, i, c], send_sem=rss.at[i, d], recv_sem=rrs.at[i, c],
            device_id={"seq": d}, device_id_type=MESH)

    def relay(buf, ssem, rsem):
        def one(y, c, part, lane_of, to):
            ref = buf.at[y, c] if part is None else buf.at[y, c, part]
            return pltpu.make_async_remote_copy(
                src_ref=ref, dst_ref=ref, send_sem=ssem.at[lane_of, c], recv_sem=rsem.at[lane_of, c],
                device_id={"mp": to}, device_id_type=MESH)

        first = lambda c: (one(m, c, None, 0, right), one(m, c, None, 1, left))
        second = lambda c: (one(left, c, 0, 2, right), one(right, c, 1, 3, left))
        got_left = lambda c: one(left, c, None, 0, right)
        got_right = lambda c: one(right, c, None, 1, left)
        got_far0 = lambda c: one(far, c, 0, 2, right)
        got_far1 = lambda c: one(far, c, 1, 3, left)

        def open_(c):
            a, b = first(c)
            a.start()
            b.start()

        def pass_on(c):
            a, b = second(c)
            got_left(c).wait_recv()
            a.start()
            got_right(c).wait_recv()
            b.start()

        def arrived(c):
            got_far0(c).wait_recv()
            got_far1(c).wait_recv()

        def drain(c):
            for cp in first(c) + second(c):
                cp.wait_send()

        return open_, pass_on, arrived, drain

    hrows = wc.shape[1] // 2

    def half(co):
        return pl.ds(pl.multiple_of(co * hrows, 16), hrows)

    def wcopy(to, y, k):
        return pltpu.make_async_remote_copy(
            src_ref=wo_ref.at[half(core), pl.ds(pl.multiple_of(to * cols, 128), cols)], dst_ref=wc.at[y, half(core)],
            send_sem=wss.at[k], recv_sem=wrs.at[k], device_id={"mp": to}, device_id_type=MESH)

    def bcopy(y, k, part):
        return pltpu.make_async_remote_copy(
            src_ref=wc.at[y, part], dst_ref=wc.at[y, part], send_sem=bss.at[k], recv_sem=brs.at[k],
            device_id={"seq": sib}, device_id_type=MESH)

    YS = [(k, lax.rem(m + k, MP), lax.rem(m + MP - k, MP)) for k in (1, 3, 2)]

    def wout_out():
        for k, to, _ in YS:
            wcopy(to, m, k).start()

    def wout_over_cores():
        for k, _, y in YS:
            wcopy(y, y, k).wait_recv()
            bcopy(y, k, half(core)).start()

    def wout_in():
        ocp.wait()
        for k, _, y in YS:
            bcopy(y, k, half(1 - core)).wait_recv()

    def wout_drain():
        for k, to, y in YS:
            wcopy(to, m, k).wait_send()
            bcopy(y, k, half(core)).wait_send()

    @pl.loop(1, NS)
    def _(k):
        mcopy(seq_at(k), s).start()

    AHEAD = 6

    @pl.loop(1, 1 + AHEAD)
    def _(t):
        zcopy(seq_at(step_k(t)), s).start()

    open1, pass1, arrived1, drain1 = relay(xg, yss, yrs)
    LAG1 = 6
    LAG2 = 12
    T0 = 10
    TM = 4

    def text_out():
        @pl.loop(1, NS)
        def _(k):
            c = seq_at(k)
            mcopy(c, c).wait()

        scp = pltpu.make_async_copy(mr, mrs, lsem.at[2])
        scp.start()
        scp.wait()

        @pl.loop(0, NS)
        def _(d):
            for i in range(2):
                ts[i, d] = text_ref[mrs[d, 0, nimg + i]]

        for i in range(2):
            tr[i, s] = ts[i, s]

        for n in range(2, 6):
            loads[n].wait()

    def norm_chunk(c):
        parts = [xg[y, c].astype(f32) for y in range(MP)]
        total = sum(jnp.sum(p, axis=-1, keepdims=True) for p in parts)
        mean = total / (MP * cols)
        parts = [p - mean for p in parts]
        var = sum(jnp.sum(p * p, axis=-1, keepdims=True) for p in parts) / (MP * cols)
        inv = lax.rsqrt(var + EPS)
        for y in range(MP):
            g = pg_ref[:, y * cols:(y + 1) * cols].reshape(1, 1, cols)
            b = pb_ref[:, y * cols:(y + 1) * cols].reshape(1, 1, cols)
            n = (parts[y] * inv * g + b).astype(bf16)
            for i in range(2):
                xn[i, c, :, y * cols:(y + 1) * cols] = n[i]

    @pl.loop(0, NS + LAG2)
    def _(t):
        @pl.when(t < NS)
        def _():
            k = step_k(t)
            c = lax.rem(s + NS - k, NS)
            d = seq_at(k)

            @pl.when(t > 0)
            def _():
                zcopy(c, c).wait_recv()

            open1(c)

            @pl.when(t > 0)
            def _():
                zcopy(d, s).wait_send()

            @pl.when((t > 0) & (t + AHEAD < NS))
            def _():
                zcopy(seq_at(step_k(t + AHEAD)), s).start()

        @pl.when((t >= T0) & (t < T0 + 8))
        def _():
            for n in range(2):
                j = 2 * (t - T0) + n

                @pl.when(j > 0)
                def _():
                    tcopy(0, seq_at(step_k(j)), s).start()

        @pl.when((t >= T0 + 8) & (t < T0 + 12))
        def _():
            for n in range(4):
                j = 4 * (t - T0 - 8) + n

                @pl.when(j > 0)
                def _():
                    tcopy(1, seq_at(step_k(j)), s).start()

        @pl.when(t == TM)
        def _():
            text_out()

        @pl.when((t >= LAG1) & (t < NS + LAG1))
        def _():
            pass1(lax.rem(s + NS - step_k(t - LAG1), NS))

        @pl.when(t >= LAG2)
        def _():
            c = lax.rem(s + NS - step_k(t - LAG2), NS)
            arrived1(c)
            norm_chunk(c)

        @pl.when(t == NS + LAG1)
        def _():
            wout_out()

    wcp.wait()
    normed = xn[...].reshape(slots, MP * cols)

    @pl.loop(0, 3)
    def _(j):
        r = jnp.dot(normed, wv[j], preferred_element_type=f32).astype(bf16)
        qkv[j] = r.reshape(qkv.shape[1:])

    span = NS * depth
    lanes = iota((1, span), 1)
    tlen = NS * depth
    for i in range(2):
        cnt = jnp.zeros((1, span), i32)
        for c in range(NS):
            cnt = jnp.where(lanes // depth == c, mrs[c, 0, 2 * s + i], cnt)
        kb[2 * i] = jnp.where(lax.rem(lanes, depth) < cnt, 0.0, NEG)
        n = len_ref[0, mrs[s, 0, nimg + i]]
        kb[2 * i + 1] = jnp.where(lanes < n, 0.0, NEG)

    scale = 1.0 / math.sqrt(HD)
    nt = (((1,), (1,)), ((), ()))

    @pl.loop(0, 2)
    def _(i):
        @pl.loop(1, NS)
        def _(k):
            c = seq_at(k)
            tcopy(i, c, c).wait_recv()

        bi = kb[2 * i]
        bt = kb[2 * i + 1]
        for h in range(heads):
            hs = slice(h * HD, (h + 1) * HD)
            q = qkv[0, i, :, hs]
            ki = qkv[1, i, :, hs]
            vi = qkv[2, i, :, hs]
            kt = tr[i, :, 0, :, hs].reshape(tlen, HD)
            vt = tr[i, :, 1, :, hs].reshape(tlen, HD)
            s1 = lax.dot_general(q, ki, nt, preferred_element_type=f32) * scale + bi
            s2 = lax.dot_general(q, kt, nt, preferred_element_type=f32) * scale + bt
            top = jnp.maximum(jnp.max(s1, axis=-1, keepdims=True), jnp.max(s2, axis=-1, keepdims=True))
            e1 = jnp.exp(s1 - top)
            e2 = jnp.exp(s2 - top)
            tot = jnp.sum(e1, axis=-1, keepdims=True) + jnp.sum(e2, axis=-1, keepdims=True)
            inv = 1.0 / tot
            p1 = (e1 * inv).astype(bf16)
            p2 = (e2 * inv).astype(bf16)
            o = jnp.dot(p1, vi, preferred_element_type=f32) + jnp.dot(p2, vt, preferred_element_type=f32)
            ret[i, :, :, hs] = o.astype(bf16).reshape(NS, depth, HD)

        ag[m, i, s] = ret[i, s]

        @pl.loop(1, NS)
        def _(t):
            rcopy(i, seq_at(step_k(t)), s).start()

    wout_over_cores()
    GS = 4
    NG = NS // GS
    LAG3 = 3

    def pass_two(i, g, src, to, n):
        ref = ag.at[src, i, pl.ds(g * GS, GS)]
        return pltpu.make_async_remote_copy(
            src_ref=ref, dst_ref=ref, send_sem=y2s.at[n, i, g], recv_sem=y2r.at[n, i, g],
            device_id={"mp": to}, device_id_type=MESH)

    def unit(u):
        i = u // NG
        v = lax.rem(u, NG)
        g = lax.rem(s // GS + jnp.where(v == 2, 3, jnp.where(v == 3, 2, v)), NG)
        odd = lax.rem(g + i, 2)
        return i, g, odd

    @pl.loop(0, 2 * NG + LAG3)
    def _(u):
        @pl.when(u < 2 * NG)
        def _():
            i, g, _ = unit(u)
            for n in range(GS):
                c = g * GS + n

                @pl.when(c != s)
                def _():
                    rcopy(i, c, c).wait_recv()

            pass_two(i, g, m, right, 0).start()
            pass_two(i, g, m, left, 1).start()

        @pl.when(u >= LAG3)
        def _():
            i, g, odd = unit(u - LAG3)
            pass_two(i, g, jnp.where(odd == 0, left, right), right, odd).wait_recv()
            pass_two(i, g, jnp.where(odd == 0, left, right), jnp.where(odd == 0, right, left), 2).start()

    wout_in()

    @pl.loop(0, 2 * NG)
    def _(u):
        i, g, odd = unit(u)
        pass_two(i, g, jnp.where(odd == 0, right, left), right, 1 - odd).wait_recv()
        pass_two(i, g, far, right, 2).wait_recv()

    eye = iota((rows, rows), 0) == iota((rows, rows), 1)

    def to_col(row):
        return jnp.sum(jnp.where(eye, jnp.broadcast_to(row, (rows, rows)), 0.0), axis=1, keepdims=True)

    def to_row(col):
        return jnp.sum(jnp.where(eye, jnp.broadcast_to(col, (rows, rows)), 0.0), axis=0, keepdims=True)

    img_f = img.astype(f32)
    pair = jnp.floor(img_f * 0.5)
    pos2 = (img_f - 2.0 * pair) * (NS * depth) + pair * depth + rank
    pick = (jnp.broadcast_to(to_col(pos2), (rows, slots)) == iota((rows, slots), 1).astype(f32)).astype(bf16)
    acc = jnp.zeros((rows, cols), f32)
    for y in range(MP):
        a = jnp.dot(pick, ag[y].reshape(slots, ag.shape[-1]), preferred_element_type=f32).astype(bf16)
        acc = acc + jnp.dot(a, wc[y], preferred_element_type=f32)

    mean = jnp.sum(acc, axis=1, keepdims=True) / cols
    dev = acc - mean
    m2 = jnp.sum(dev * dev, axis=1, keepdims=True)
    st[0:1, :] = to_row(mean)
    st[1:2, :] = to_row(m2)

    def scopy(k, to):
        return pltpu.make_async_remote_copy(
            src_ref=st, dst_ref=sr.at[k], send_sem=sss.at[k], recv_sem=srs.at[k],
            device_id={"mp": to}, device_id_type=MESH)

    for k in (1, 3, 2):
        scopy(k, lax.rem(m + k, MP)).start()

    @pl.loop(1, NS)
    def _(k):
        d = seq_at(k)
        for i in range(2):
            tcopy(i, d, s).wait_send()
            rcopy(i, d, s).wait_send()

    @pl.loop(0, NS)
    def _(c):
        drain1(c)

    @pl.loop(0, NG)
    def _(g):
        for i in range(2):
            for n in range(3):
                pass_two(i, g, m, right, n).wait_send()

    wout_drain()

    for k in (1, 3, 2):
        scopy(k, lax.rem(m + k, MP)).wait()

    means = [st[0:1, :]] + [sr[k, 0:1, :] for k in (1, 2, 3)]
    m2s = [st[1:2, :]] + [sr[k, 1:2, :] for k in (1, 2, 3)]
    avg = sum(means) / MP
    sq = sum(m2s) + cols * sum((u - avg) * (u - avg) for u in means)
    rstd = lax.rsqrt(sq / (MP * cols) + EPS)
    avg_c = to_col(avg)
    rstd_c = to_col(rstd)
    own = pl.ds(pl.multiple_of(m * cols, 128), cols)
    n = (acc - avg_c) * rstd_c * qg_ref[:, own] + qb_ref[:, own]
    o_ref[...] = (x_ref[...].astype(f32) + n).astype(bf16)


def shards(
    patches, image_of, prompt_of, text_len, text_kv, w_qkv, w_out, pre_gain, pre_bias, post_gain, post_bias,
):
    NS = lax.axis_size("seq")
    MP = lax.axis_size("mp")
    rows, cols = patches.shape
    depth = rows // NS
    hc = w_out.shape[0]
    toks = text_kv.shape[1]
    text = jnp.transpose(text_kv, (0, 2, 1, 3))
    w = jnp.transpose(w_qkv, (1, 0, 2))
    full = w_qkv.shape[0]
    vm = pl.BlockSpec(memory_space=pltpu.VMEM)
    sm = pl.BlockSpec(memory_space=pltpu.SMEM)
    anys = pl.BlockSpec(memory_space=pl.ANY)
    dma = pltpu.SemaphoreType.DMA
    return pl.pallas_call(
        fused,
        out_shape=jax.ShapeDtypeStruct((rows, cols), bf16),
        in_specs=[anys, anys, sm, sm, vm, anys, anys, anys, anys, anys, anys],
        out_specs=vm,
        scratch_shapes=[
            pltpu.VMEM((rows, cols), bf16),
            pltpu.VMEM((1, rows), i32),
            pltpu.VMEM((1, full), f32),
            pltpu.VMEM((1, full), f32),
            pltpu.VMEM((1, full), f32),
            pltpu.VMEM((1, full), f32),
            pltpu.VMEM((NS, 2, depth, cols), bf16),
            pltpu.VMEM((MP, NS, 2, depth, cols), bf16),
            pltpu.VMEM((2, NS, depth, full), bf16),
            pltpu.VMEM((3, full, hc), bf16),
            pltpu.VMEM((MP, hc, cols), bf16),
            pltpu.VMEM((3, 2, NS * depth, hc), bf16),
            pltpu.VMEM((2, NS, 2, toks, hc), bf16),
            pltpu.VMEM((2, NS, 2, toks, hc), bf16),
            pltpu.VMEM((2, NS, depth, hc), bf16),
            pltpu.VMEM((MP, 2, NS, depth, hc), bf16),
            pltpu.VMEM((1, 128), i32),
            pltpu.VMEM((NS, 1, 128), i32),
            pltpu.SMEM((NS, 1, 128), i32),
            pltpu.VMEM((8, rows), f32),
            pltpu.VMEM((MP, 8, rows), f32),
            pltpu.VMEM((4, 1, NS * depth), f32),
            dma((NS,)), dma((NS,)), dma((2, NS)), dma((2, NS)), dma((NS,)), dma((NS,)),
            dma((4, NS)), dma((4, NS)), dma((2, NS)), dma((2, NS)), dma((3, 2, NS // 4)), dma((3, 2, NS // 4)),
            dma((MP,)), dma((MP,)), dma((MP,)), dma((MP,)), dma((MP,)), dma((MP,)),
            dma((9,)),
        ],
        compiler_params=pltpu.CompilerParams(collective_id=0, has_side_effects=True, vmem_limit_bytes=58 << 20),
    )(
        patches, image_of.reshape(1, rows), prompt_of, text_len, text, w, w_out,
        pre_gain.reshape(1, -1), pre_bias.reshape(1, -1), post_gain.reshape(1, -1), post_bias.reshape(1, -1),
    )


def solution(mesh):
    placed = (
        P(("dp", "seq"), "mp"),
        P(("dp", "seq")),
        P("dp", "seq"),
        P("dp", None),
        P("dp", "seq", None, "mp"),
        P(None, None, "mp"),
        P("mp", None),
        P(),
        P(),
        P(),
        P(),
    )
    return jax.shard_map(
        shards, mesh=mesh, in_specs=placed, out_specs=P(("dp", "seq"), "mp"), check_vma=False
    )
```

```python
import math

import jax
import jax.numpy as jnp
from jax import lax
from jax.experimental import pallas as pl
from jax.experimental.pallas import tpu as pltpu
from jax.sharding import PartitionSpec as P

HD = 128
EPS = 1e-05
MESH = pl.DeviceIdType.MESH
NEG = -1e30

f32 = jnp.float32
bf16 = jnp.bfloat16
i32 = jnp.int32


def iota(shape, dim):
    return lax.broadcasted_iota(i32, shape, dim)


def fused(
    x_in, img_in, prm_ref, len_ref, text_ref, w_ref, wo_ref, pg_in, pb_in, qg_in, qb_in,
    o_ref,
    x_ref, img_ref, pg_ref, pb_ref, qg_ref, qb_ref, xs, xg, xn, wv, wc, qkv, ts, tr, ret, rb, av, ms, mr, mrs, st, sr, kb,
    zss, zrs, tss, trs, mss, mrsem, yss, yrs, rss, rrs, y2s, y2r, wss, wrs, bss, brs, sss, srs, lsem,
):
    s = lax.axis_index("seq")
    m = lax.axis_index("mp")
    NS, MP = xg.shape[1], xg.shape[0]
    rows = x_ref.shape[0]
    cols = x_ref.shape[1]
    slots = xs.shape[2] * xs.shape[1] * NS
    depth = xs.shape[2]
    nimg = 2 * NS
    heads = qkv.shape[-1] // HD
    right = lax.rem(m + 1, MP)
    left = lax.rem(m + MP - 1, MP)
    far = lax.rem(m + 2, MP)
    core = lax.rem(s, 2)
    sib = s + 1 - 2 * core

    NP = NS // 2
    pair = s // 2

    def seq_at(k):
        return lax.rem(s + k, NS)

    def hop(v):
        far_by = (v + 1) // 2
        return jnp.where(lax.rem(v, 2) == 1, far_by, NP - far_by)

    def to_pair(v):
        return lax.rem(pair + hop(v), NP)

    def from_pair(v):
        return lax.rem(pair + 2 * NP - hop(v), NP)

    def source(r):
        return 2 * from_pair(r // 2) + lax.rem(r + core, 2)

    bar = pltpu.get_barrier_semaphore()

    @pl.loop(1, NS)
    def _(k):
        pl.semaphore_signal(bar, inc=1, device_id={"seq": seq_at(k)}, device_id_type=MESH)

    for d in (right, left, far):
        pl.semaphore_signal(bar, inc=1, device_id={"mp": d}, device_id_type=MESH)

    loads = []
    for n, (a, b) in enumerate(
        ((img_in, img_ref), (x_in, x_ref), (pg_in, pg_ref), (pb_in, pb_ref), (qg_in, qg_ref), (qb_in, qb_ref))
    ):
        loads.append(pltpu.make_async_copy(a, b, lsem.at[3 + n]))
        loads[-1].start()
    wcp = pltpu.make_async_copy(w_ref, wv, lsem.at[0])
    wcp.start()
    ocp = pltpu.make_async_copy(wo_ref.at[:, pl.ds(pl.multiple_of(m * cols, 128), cols)], wc.at[m], lsem.at[1])
    ocp.start()

    loads[0].wait()
    img = img_ref[...]
    onehot = (jnp.broadcast_to(img, (nimg, rows)) == iota((nimg, rows), 0)).astype(f32)
    upto = (iota((rows, rows), 0) <= iota((rows, rows), 1)).astype(bf16)
    cum = jnp.dot(onehot.astype(bf16), upto, preferred_element_type=f32)
    rank = jnp.sum(cum * onehot, axis=0, keepdims=True) - 1.0
    pos = img.astype(f32) * depth + rank
    counts = jnp.sum(onehot, axis=1, keepdims=True)
    crow = jnp.sum(
        jnp.where(iota((nimg, 128), 0) == iota((nimg, 128), 1), jnp.broadcast_to(counts, (nimg, 128)), 0.0),
        axis=0, keepdims=True,
    ).astype(i32)
    lane = iota((1, 128), 1)
    crow = jnp.where(lane == nimg, prm_ref[0, 0], jnp.where(lane == nimg + 1, prm_ref[0, 1], crow))
    ms[...] = crow
    mr[s] = crow
    place = (jnp.broadcast_to(pos, (slots, rows)) == iota((slots, rows), 0).astype(f32)).astype(bf16)
    loads[1].wait()
    spread = jnp.dot(place, x_ref[...], preferred_element_type=f32).astype(bf16)
    xs[...] = spread.reshape(xs.shape)
    xg[m, s] = xs[s]

    pl.semaphore_wait(bar, NS - 1 + MP - 1)

    def copy(src, dst, ss, rs, **to):
        return pltpu.make_async_remote_copy(
            src_ref=src, dst_ref=dst, send_sem=ss, recv_sem=rs, device_id=to, device_id_type=MESH)

    def zcopy(d):
        return copy(xs.at[d], xg.at[m, s], zss.at[0], zrs.at[s], seq=d)

    def zgot(c):
        copy(xg.at[m, c], xg.at[m, c], zss.at[0], zrs.at[c], seq=sib).wait_recv()

    def tcopy(i, d):
        return copy(ts.at[i, d], tr.at[i, s], tss.at[i], trs.at[i], seq=d)

    def mcopy(d):
        return copy(ms, mr.at[s], mss.at[0], mrsem.at[0], seq=d)

    def rcopy(h, r, d):
        return copy(ret.at[h, r], rb.at[h, s], rss.at[h], rrs.at[h], seq=d)

    def acopy(h, to):
        return copy(av.at[m, h], av.at[m, h], y2s.at[0], y2r.at[m], mp=to)

    most = pl.ds(0, NS - 1)

    def each_other(start):
        @pl.loop(1, NS)
        def _(r):
            start(2 * to_pair(r // 2) + lax.rem(r + core, 2)).start()

    def unit1(y, c, n, to):
        ref = xg.at[y, c] if n < 2 else xg.at[y, c, n - 2]
        return copy(ref, ref, yss.at[n], yrs.at[n, c], mp=to)

    def open1(j):
        unit1(m, j, 0, right).start()
        unit1(m, j, 1, left).start()

    def pass1(j):
        unit1(left, j, 0, right).wait_recv()
        unit1(left, j, 2, right).start()
        unit1(right, j, 1, left).wait_recv()
        unit1(right, j, 3, left).start()

    def arrived1(j):
        unit1(far, j, 2, right).wait_recv()
        unit1(far, j, 3, left).wait_recv()

    def drain1():
        for n in range(4):
            ref = xg.at[m] if n < 2 else xg.at[m, pl.ds(0, NP)]
            copy(ref, ref, yss.at[n], yrs.at[n, 0], mp=right).wait_send()

    hrows = wc.shape[1] // 2

    def half(co):
        return pl.ds(pl.multiple_of(co * hrows, 16), hrows)

    def wcopy(to, y, k):
        return pltpu.make_async_remote_copy(
            src_ref=wo_ref.at[half(core), pl.ds(pl.multiple_of(to * cols, 128), cols)], dst_ref=wc.at[y, half(core)],
            send_sem=wss.at[k], recv_sem=wrs.at[k], device_id={"mp": to}, device_id_type=MESH)

    def bcopy(y, k, part):
        return pltpu.make_async_remote_copy(
            src_ref=wc.at[y, part], dst_ref=wc.at[y, part], send_sem=bss.at[k], recv_sem=brs.at[k],
            device_id={"seq": sib}, device_id_type=MESH)

    YS = [(k, lax.rem(m + k, MP), lax.rem(m + MP - k, MP)) for k in (1, 3, 2)]

    def wout_out():
        for k, to, _ in YS:
            wcopy(to, m, k).start()

    def wout_over_cores():
        for k, _, y in YS:
            wcopy(y, y, k).wait_recv()
            bcopy(y, k, half(core)).start()

    def wout_in():
        ocp.wait()
        for k, _, y in YS:
            bcopy(y, k, half(1 - core)).wait_recv()

    def wout_drain():
        for k, to, y in YS:
            wcopy(to, m, k).wait_send()
            bcopy(y, k, half(core)).wait_send()

    each_other(mcopy)
    each_other(zcopy)

    LAG1 = 6
    LAG2 = 12
    TM = 4
    T0 = 8
    T1 = 14

    def text_out():
        copy(mr.at[most], mr.at[most], mss.at[0], mrsem.at[0], seq=sib).wait_recv()
        scp = pltpu.make_async_copy(mr, mrs, lsem.at[2])
        scp.start()
        scp.wait()

        @pl.loop(0, NS)
        def _(d):
            for i in range(2):
                ts[i, d] = text_ref[mrs[d, 0, nimg + i]]

        for i in range(2):
            tr[i, s] = ts[i, s]

        for n in range(2, 6):
            loads[n].wait()
        wcp.wait()

    def project(hf, j):
        r = jnp.dot(xn[hf].reshape(slots // 2, MP * cols), wv[j], preferred_element_type=f32).astype(bf16)
        qkv[j, :, hf] = r.reshape(2, slots // 4, r.shape[-1])

    def norm_chunk(c, hf, r):
        parts = [xg[y, c].astype(f32) for y in range(MP)]
        total = sum(jnp.sum(p, axis=-1, keepdims=True) for p in parts)
        mean = total / (MP * cols)
        parts = [p - mean for p in parts]
        var = sum(jnp.sum(p * p, axis=-1, keepdims=True) for p in parts) / (MP * cols)
        inv = lax.rsqrt(var + EPS)
        for y in range(MP):
            g = pg_ref[:, y * cols:(y + 1) * cols].reshape(1, 1, cols)
            b = pb_ref[:, y * cols:(y + 1) * cols].reshape(1, 1, cols)
            n = (parts[y] * inv * g + b).astype(bf16)
            for i in range(2):
                xn[hf, i, r, :, y * cols:(y + 1) * cols] = n[i]

    @pl.loop(0, NS + LAG2)
    def _(t):
        @pl.when((t > 0) & (t < NS))
        def _():
            zgot(source(t))

        @pl.when(t < NS)
        def _():
            open1(source(t))

        @pl.when(t == TM)
        def _():
            text_out()

        @pl.when(t == T0)
        def _():
            each_other(lambda d: tcopy(0, d))

        @pl.when(t == T1)
        def _():
            each_other(lambda d: tcopy(1, d))

        @pl.when((t >= LAG1) & (t < NS + LAG1))
        def _():
            pass1(source(t - LAG1))

        @pl.when(t == NS + LAG1)
        def _():
            wout_out()

        @pl.when(t >= LAG2)
        def _():
            c = source(t - LAG2)
            arrived1(c)
            norm_chunk(c, (t - LAG2) // NP, lax.rem(t - LAG2, NP))

        @pl.when((t >= LAG2 + NP - 1) & (t < LAG2 + NP + 2))
        def _():
            project(0, t - (LAG2 + NP - 1))

    @pl.loop(0, 3)
    def _(j):
        project(1, j)

    span = NS * depth
    lanes = iota((1, span), 1)
    tlen = NS * depth
    for i in range(2):
        cnt = jnp.zeros((1, span), i32)
        for r in range(NS):
            cnt = jnp.where(lanes // depth == r, mrs[source(r), 0, 2 * s + i], cnt)
        kb[2 * i] = jnp.where(lax.rem(lanes, depth) < cnt, 0.0, NEG)
        n = len_ref[0, mrs[s, 0, nimg + i]]
        kb[2 * i + 1] = jnp.where(lanes < n, 0.0, NEG)

    scale = 1.0 / math.sqrt(HD)
    nt = (((1,), (1,)), ((), ()))
    for i in range(2):
        copy(tr.at[i, most], tr.at[i, most], tss.at[i], trs.at[i], seq=sib).wait_recv()

    for h in range(heads):
        hs = slice(h * HD, (h + 1) * HD)

        @pl.loop(0, 2)
        def _(i):
            bi = kb[2 * i]
            bt = kb[2 * i + 1]
            q, ki, vi = (qkv[n, i, :, :, hs].reshape(tlen, HD) for n in range(3))
            kt = tr[i, :, 0, :, hs].reshape(tlen, HD)
            vt = tr[i, :, 1, :, hs].reshape(tlen, HD)
            s1 = lax.dot_general(q, ki, nt, preferred_element_type=f32) * scale + bi
            s2 = lax.dot_general(q, kt, nt, preferred_element_type=f32) * scale + bt
            top = jnp.maximum(jnp.max(s1, axis=-1, keepdims=True), jnp.max(s2, axis=-1, keepdims=True))
            e1 = jnp.exp(s1 - top)
            e2 = jnp.exp(s2 - top)
            tot = jnp.sum(e1, axis=-1, keepdims=True) + jnp.sum(e2, axis=-1, keepdims=True)
            inv = 1.0 / tot
            p1 = (e1 * inv).astype(bf16)
            p2 = (e2 * inv).astype(bf16)
            o = jnp.dot(p1, vi, preferred_element_type=f32) + jnp.dot(p2, vt, preferred_element_type=f32)
            ret[h, :, i] = o.astype(bf16).reshape(NS, depth, HD)

        rb[h, s] = ret[h, 0]

        @pl.loop(1, NS)
        def _(r):
            rcopy(h, r, source(r)).start()

    eye = iota((rows, rows), 0) == iota((rows, rows), 1)

    def to_col(row):
        return jnp.sum(jnp.where(eye, jnp.broadcast_to(row, (rows, rows)), 0.0), axis=1, keepdims=True)

    def to_row(col):
        return jnp.sum(jnp.where(eye, jnp.broadcast_to(col, (rows, rows)), 0.0), axis=0, keepdims=True)

    pick = (jnp.broadcast_to(to_col(pos), (rows, slots)) == iota((rows, slots), 1).astype(f32)).astype(bf16)
    wout_over_cores()
    for h in range(heads):
        copy(rb.at[h, most], rb.at[h, most], rss.at[h], rrs.at[h], seq=sib).wait_recv()
        av[m, h] = jnp.dot(pick, rb[h].reshape(slots, HD), preferred_element_type=f32).astype(bf16)
        for to in (right, left, far):
            acopy(h, to).start()

    wout_in()

    def part(y):
        a = jnp.concatenate([av[y, h] for h in range(heads)], axis=1)
        return jnp.dot(a, wc[y], preferred_element_type=f32)

    acc = part(m)
    for y in (right, left, far):
        copy(av.at[y], av.at[y], y2s.at[0], y2r.at[y], mp=right).wait_recv()
        acc = acc + part(y)

    mean = jnp.sum(acc, axis=1, keepdims=True) / cols
    dev = acc - mean
    m2 = jnp.sum(dev * dev, axis=1, keepdims=True)
    st[0:1, :] = to_row(mean)
    st[1:2, :] = to_row(m2)

    def scopy(k, to):
        return pltpu.make_async_remote_copy(
            src_ref=st, dst_ref=sr.at[k], send_sem=sss.at[k], recv_sem=srs.at[k],
            device_id={"mp": to}, device_id_type=MESH)

    for k in (1, 3, 2):
        scopy(k, lax.rem(m + k, MP)).start()

    copy(mr.at[most], mr.at[most], mss.at[0], mrsem.at[0], seq=sib).wait_send()
    copy(xs.at[most], xs.at[most], zss.at[0], zrs.at[0], seq=sib).wait_send()
    for i in range(2):
        copy(ts.at[i, most], ts.at[i, most], tss.at[i], trs.at[i], seq=sib).wait_send()
    for h in range(heads):
        copy(ret.at[h, most], ret.at[h, most], rss.at[h], rrs.at[h], seq=sib).wait_send()
    drain1()
    copy(av.at[pl.ds(0, MP - 1)], av.at[pl.ds(0, MP - 1)], y2s.at[0], y2r.at[0], mp=right).wait_send()
    wout_drain()

    for k in (1, 3, 2):
        scopy(k, lax.rem(m + k, MP)).wait()

    means = [st[0:1, :]] + [sr[k, 0:1, :] for k in (1, 2, 3)]
    m2s = [st[1:2, :]] + [sr[k, 1:2, :] for k in (1, 2, 3)]
    avg = sum(means) / MP
    sq = sum(m2s) + cols * sum((u - avg) * (u - avg) for u in means)
    rstd = lax.rsqrt(sq / (MP * cols) + EPS)
    avg_c = to_col(avg)
    rstd_c = to_col(rstd)
    own = pl.ds(pl.multiple_of(m * cols, 128), cols)
    n = (acc - avg_c) * rstd_c * qg_ref[:, own] + qb_ref[:, own]
    o_ref[...] = (x_ref[...].astype(f32) + n).astype(bf16)


def shards(
    patches, image_of, prompt_of, text_len, text_kv, w_qkv, w_out, pre_gain, pre_bias, post_gain, post_bias,
):
    NS = lax.axis_size("seq")
    MP = lax.axis_size("mp")
    rows, cols = patches.shape
    depth = rows // NS
    hc = w_out.shape[0]
    toks = text_kv.shape[1]
    heads = hc // HD
    text = jnp.transpose(text_kv, (0, 2, 1, 3))
    w = jnp.transpose(w_qkv, (1, 0, 2))
    full = w_qkv.shape[0]
    vm = pl.BlockSpec(memory_space=pltpu.VMEM)
    sm = pl.BlockSpec(memory_space=pltpu.SMEM)
    anys = pl.BlockSpec(memory_space=pl.ANY)
    dma = pltpu.SemaphoreType.DMA
    return pl.pallas_call(
        fused,
        out_shape=jax.ShapeDtypeStruct((rows, cols), bf16),
        in_specs=[anys, anys, sm, sm, vm, anys, anys, anys, anys, anys, anys],
        out_specs=vm,
        scratch_shapes=[
            pltpu.VMEM((rows, cols), bf16),
            pltpu.VMEM((1, rows), i32),
            pltpu.VMEM((1, full), f32),
            pltpu.VMEM((1, full), f32),
            pltpu.VMEM((1, full), f32),
            pltpu.VMEM((1, full), f32),
            pltpu.VMEM((NS, 2, depth, cols), bf16),
            pltpu.VMEM((MP, NS, 2, depth, cols), bf16),
            pltpu.VMEM((2, 2, NS // 2, depth, full), bf16),
            pltpu.VMEM((3, full, hc), bf16),
            pltpu.VMEM((MP, hc, cols), bf16),
            pltpu.VMEM((3, 2, 2, NS * depth // 2, hc), bf16),
            pltpu.VMEM((2, NS, 2, toks, hc), bf16),
            pltpu.VMEM((2, NS, 2, toks, hc), bf16),
            pltpu.VMEM((heads, NS, 2, depth, HD), bf16),
            pltpu.VMEM((heads, NS, 2, depth, HD), bf16),
            pltpu.VMEM((MP, heads, rows, HD), bf16),
            pltpu.VMEM((1, 128), i32),
            pltpu.VMEM((NS, 1, 128), i32),
            pltpu.SMEM((NS, 1, 128), i32),
            pltpu.VMEM((8, rows), f32),
            pltpu.VMEM((MP, 8, rows), f32),
            pltpu.VMEM((4, 1, NS * depth), f32),
            dma((1,)), dma((NS,)), dma((2,)), dma((2,)), dma((1,)), dma((1,)),
            dma((4,)), dma((4, NS)), dma((heads,)), dma((heads,)), dma((1,)), dma((MP,)),
            dma((MP,)), dma((MP,)), dma((MP,)), dma((MP,)), dma((MP,)), dma((MP,)),
            dma((9,)),
        ],
        compiler_params=pltpu.CompilerParams(collective_id=0, has_side_effects=True, vmem_limit_bytes=58 << 20),
    )(
        patches, image_of.reshape(1, rows), prompt_of, text_len, text, w, w_out,
        pre_gain.reshape(1, -1), pre_bias.reshape(1, -1), post_gain.reshape(1, -1), post_bias.reshape(1, -1),
    )


def solution(mesh):
    placed = (
        P(("dp", "seq"), "mp"),
        P(("dp", "seq")),
        P("dp", "seq"),
        P("dp", None),
        P("dp", "seq", None, "mp"),
        P(None, None, "mp"),
        P("mp", None),
        P(),
        P(),
        P(),
        P(),
    )
    return jax.shard_map(
        shards, mesh=mesh, in_specs=placed, out_specs=P(("dp", "seq"), "mp"), check_vma=False
    )
```

```python
import math

import jax
import jax.numpy as jnp
from jax import lax
from jax.experimental import pallas as pl
from jax.experimental.pallas import tpu as pltpu
from jax.sharding import PartitionSpec as P

HD = 128
EPS = 1e-05
MESH = pl.DeviceIdType.MESH
NEG = -1e30

f32 = jnp.float32
bf16 = jnp.bfloat16
i32 = jnp.int32


def iota(shape, dim):
    return lax.broadcasted_iota(i32, shape, dim)


def fused(
    x_in, img_in, prm_ref, len_ref, text_ref, w_ref, wo_ref, pg_in, pb_in, qg_in, qb_in,
    o_ref,
    x_ref, img_ref, pg_ref, pb_ref, qg_ref, qb_ref, xs, xg, xn, wv, wc, qkv, ts, tr, ret, rb, av, tx, ms, mr, mrs, st, sr, kb,
    zss, zrs, tss, trs, mss, mrsem, yss, yrs, rss, rrs, y2s, y2r, wss, wrs, bss, brs, sss, srs, lsem,
):
    s = lax.axis_index("seq")
    m = lax.axis_index("mp")
    NS, MP = xg.shape[1], xg.shape[0]
    rows = x_ref.shape[0]
    cols = x_ref.shape[1]
    slots = xs.shape[2] * xs.shape[1] * NS
    depth = xs.shape[2]
    nimg = 2 * NS
    heads = qkv.shape[-1] // HD
    right = lax.rem(m + 1, MP)
    left = lax.rem(m + MP - 1, MP)
    far = lax.rem(m + 2, MP)
    core = lax.rem(s, 2)
    sib = s + 1 - 2 * core

    NP = NS // 2
    pair = s // 2

    def seq_at(k):
        return lax.rem(s + k, NS)

    def hop(v):
        far_by = (v + 1) // 2
        return jnp.where(lax.rem(v, 2) == 1, far_by, NP - far_by)

    def to_pair(v):
        return lax.rem(pair + hop(v), NP)

    def from_pair(v):
        return lax.rem(pair + 2 * NP - hop(v), NP)

    def source(r):
        return 2 * from_pair(r // 2) + lax.rem(r + core, 2)

    bar = pltpu.get_barrier_semaphore()

    @pl.loop(1, NS)
    def _(k):
        pl.semaphore_signal(bar, inc=1, device_id={"seq": seq_at(k)}, device_id_type=MESH)

    for d in (right, left, far):
        pl.semaphore_signal(bar, inc=1, device_id={"mp": d}, device_id_type=MESH)

    loads = []
    for n, (a, b) in enumerate(
        ((img_in, img_ref), (x_in, x_ref), (pg_in, pg_ref), (pb_in, pb_ref), (qg_in, qg_ref), (qb_in, qb_ref), (text_ref, tx))
    ):
        loads.append(pltpu.make_async_copy(a, b, lsem.at[3 + n]))
        loads[-1].start()
    wcp = pltpu.make_async_copy(w_ref, wv, lsem.at[0])
    wcp.start()
    ocp = pltpu.make_async_copy(wo_ref.at[:, pl.ds(pl.multiple_of(m * cols, 128), cols)], wc.at[m], lsem.at[1])
    ocp.start()

    loads[0].wait()
    img = img_ref[...]
    onehot = (jnp.broadcast_to(img, (nimg, rows)) == iota((nimg, rows), 0)).astype(f32)
    upto = (iota((rows, rows), 0) <= iota((rows, rows), 1)).astype(bf16)
    cum = jnp.dot(onehot.astype(bf16), upto, preferred_element_type=f32)
    rank = jnp.sum(cum * onehot, axis=0, keepdims=True) - 1.0
    pos = img.astype(f32) * depth + rank
    counts = jnp.sum(onehot, axis=1, keepdims=True)
    crow = jnp.sum(
        jnp.where(iota((nimg, 128), 0) == iota((nimg, 128), 1), jnp.broadcast_to(counts, (nimg, 128)), 0.0),
        axis=0, keepdims=True,
    ).astype(i32)
    lane = iota((1, 128), 1)
    crow = jnp.where(lane == nimg, prm_ref[0, 0], jnp.where(lane == nimg + 1, prm_ref[0, 1], crow))
    ms[...] = crow
    mr[s] = crow
    place = (jnp.broadcast_to(pos, (slots, rows)) == iota((slots, rows), 0).astype(f32)).astype(bf16)
    loads[1].wait()
    spread = jnp.dot(place, x_ref[...], preferred_element_type=f32).astype(bf16)
    xs[...] = spread.reshape(xs.shape)
    xg[m, s] = xs[s]

    pl.semaphore_wait(bar, NS - 1 + MP - 1)

    def copy(src, dst, ss, rs, **to):
        return pltpu.make_async_remote_copy(
            src_ref=src, dst_ref=dst, send_sem=ss, recv_sem=rs, device_id=to, device_id_type=MESH)

    def zcopy(d):
        return copy(xs.at[d], xg.at[m, s], zss.at[0], zrs.at[s], seq=d)

    def zgot(c):
        copy(xg.at[m, c], xg.at[m, c], zss.at[0], zrs.at[c], seq=sib).wait_recv()

    def tcopy(i, d):
        return copy(ts.at[i, d], tr.at[i, s], tss.at[i], trs.at[i], seq=d)

    def mcopy(d):
        return copy(ms, mr.at[s], mss.at[0], mrsem.at[0], seq=d)

    def rcopy(h, r, d):
        return copy(ret.at[h, r], rb.at[h, s], rss.at[h], rrs.at[h], seq=d)

    def acopy(h, to):
        return copy(av.at[m, h], av.at[m, h], y2s.at[0], y2r.at[m], mp=to)

    most = pl.ds(0, NS - 1)

    def each_other(start):
        @pl.loop(1, NS)
        def _(r):
            start(2 * to_pair(r // 2) + lax.rem(r + core, 2)).start()

    def unit1(y, c, n, to):
        ref = xg.at[y, c] if n < 2 else xg.at[y, c, n - 2]
        return copy(ref, ref, yss.at[n], yrs.at[n, c], mp=to)

    def open1(j):
        unit1(m, j, 0, right).start()
        unit1(m, j, 1, left).start()

    def pass1(j):
        unit1(left, j, 0, right).wait_recv()
        unit1(left, j, 2, right).start()
        unit1(right, j, 1, left).wait_recv()
        unit1(right, j, 3, left).start()

    def arrived1(j):
        unit1(far, j, 2, right).wait_recv()
        unit1(far, j, 3, left).wait_recv()

    def drain1():
        for n in range(4):
            ref = xg.at[m] if n < 2 else xg.at[m, pl.ds(0, NP)]
            copy(ref, ref, yss.at[n], yrs.at[n, 0], mp=right).wait_send()

    hrows = wc.shape[1] // 2

    def half(co):
        return pl.ds(pl.multiple_of(co * hrows, 16), hrows)

    def wcopy(to, y, k):
        return pltpu.make_async_remote_copy(
            src_ref=wo_ref.at[half(core), pl.ds(pl.multiple_of(to * cols, 128), cols)], dst_ref=wc.at[y, half(core)],
            send_sem=wss.at[k], recv_sem=wrs.at[k], device_id={"mp": to}, device_id_type=MESH)

    def bcopy(y, k, part):
        return pltpu.make_async_remote_copy(
            src_ref=wc.at[y, part], dst_ref=wc.at[y, part], send_sem=bss.at[k], recv_sem=brs.at[k],
            device_id={"seq": sib}, device_id_type=MESH)

    YS = [(k, lax.rem(m + k, MP), lax.rem(m + MP - k, MP)) for k in (1, 3, 2)]

    def wout_out():
        for k, to, _ in YS:
            wcopy(to, m, k).start()

    def wout_over_cores():
        for k, _, y in YS:
            wcopy(y, y, k).wait_recv()
            bcopy(y, k, half(core)).start()

    def wout_in():
        ocp.wait()
        for k, _, y in YS:
            bcopy(y, k, half(1 - core)).wait_recv()

    def wout_drain():
        for k, to, y in YS:
            wcopy(to, m, k).wait_send()
            bcopy(y, k, half(core)).wait_send()

    each_other(mcopy)
    each_other(zcopy)

    LAG1 = 6
    LAG2 = 12
    TM = 4
    T0 = 8
    T1 = 14

    def text_out():
        loads[6].wait()
        copy(mr.at[most], mr.at[most], mss.at[0], mrsem.at[0], seq=sib).wait_recv()
        scp = pltpu.make_async_copy(mr, mrs, lsem.at[2])
        scp.start()
        scp.wait()

        @pl.loop(0, NS)
        def _(d):
            for i in range(2):
                both = tx[mrs[d, 0, nimg + i]]
                ts[i, d, 0] = both[:, 0, :]
                ts[i, d, 1] = both[:, 1, :]

        for i in range(2):
            tr[i, s] = ts[i, s]

        for n in range(2, 6):
            loads[n].wait()
        wcp.wait()

    def project(hf, j):
        r = jnp.dot(xn[hf].reshape(slots // 2, MP * cols), wv[j], preferred_element_type=f32).astype(bf16)
        qkv[j, :, hf] = r.reshape(2, slots // 4, r.shape[-1])

    def norm_chunk(c, hf, r):
        parts = [xg[y, c].astype(f32) for y in range(MP)]
        total = sum(jnp.sum(p, axis=-1, keepdims=True) for p in parts)
        mean = total / (MP * cols)
        parts = [p - mean for p in parts]
        var = sum(jnp.sum(p * p, axis=-1, keepdims=True) for p in parts) / (MP * cols)
        inv = lax.rsqrt(var + EPS)
        for y in range(MP):
            g = pg_ref[:, y * cols:(y + 1) * cols].reshape(1, 1, cols)
            b = pb_ref[:, y * cols:(y + 1) * cols].reshape(1, 1, cols)
            n = (parts[y] * inv * g + b).astype(bf16)
            for i in range(2):
                xn[hf, i, r, :, y * cols:(y + 1) * cols] = n[i]

    @pl.loop(0, NS + LAG2)
    def _(t):
        @pl.when((t > 0) & (t < NS))
        def _():
            zgot(source(t))

        @pl.when(t < NS)
        def _():
            open1(source(t))

        @pl.when(t == TM)
        def _():
            text_out()

        @pl.when(t == T0)
        def _():
            each_other(lambda d: tcopy(0, d))

        @pl.when(t == T1)
        def _():
            each_other(lambda d: tcopy(1, d))

        @pl.when((t >= LAG1) & (t < NS + LAG1))
        def _():
            pass1(source(t - LAG1))

        @pl.when(t == NS + LAG1)
        def _():
            wout_out()

        @pl.when(t >= LAG2)
        def _():
            c = source(t - LAG2)
            arrived1(c)
            norm_chunk(c, (t - LAG2) // NP, lax.rem(t - LAG2, NP))

        @pl.when((t >= LAG2 + NP - 1) & (t < LAG2 + NP + 2))
        def _():
            project(0, t - (LAG2 + NP - 1))

    @pl.loop(0, 3)
    def _(j):
        project(1, j)

    span = NS * depth
    lanes = iota((1, span), 1)
    tlen = NS * depth
    for i in range(2):
        cnt = jnp.zeros((1, span), i32)
        for r in range(NS):
            cnt = jnp.where(lanes // depth == r, mrs[source(r), 0, 2 * s + i], cnt)
        kb[2 * i] = jnp.where(lax.rem(lanes, depth) < cnt, 0.0, NEG)
        n = len_ref[0, mrs[s, 0, nimg + i]]
        kb[2 * i + 1] = jnp.where(lanes < n, 0.0, NEG)

    scale = 1.0 / math.sqrt(HD)
    nt = (((1,), (1,)), ((), ()))
    for i in range(2):
        copy(tr.at[i, most], tr.at[i, most], tss.at[i], trs.at[i], seq=sib).wait_recv()

    for h in range(heads):
        hs = slice(h * HD, (h + 1) * HD)

        @pl.loop(0, 2)
        def _(i):
            bi = kb[2 * i]
            bt = kb[2 * i + 1]
            q, ki, vi = (qkv[n, i, :, :, hs].reshape(tlen, HD) for n in range(3))
            kt = tr[i, :, 0, :, hs].reshape(tlen, HD)
            vt = tr[i, :, 1, :, hs].reshape(tlen, HD)
            s1 = lax.dot_general(q, ki, nt, preferred_element_type=f32) * scale + bi
            s2 = lax.dot_general(q, kt, nt, preferred_element_type=f32) * scale + bt
            top = jnp.maximum(jnp.max(s1, axis=-1, keepdims=True), jnp.max(s2, axis=-1, keepdims=True))
            e1 = jnp.exp(s1 - top)
            e2 = jnp.exp(s2 - top)
            tot = jnp.sum(e1, axis=-1, keepdims=True) + jnp.sum(e2, axis=-1, keepdims=True)
            inv = 1.0 / tot
            p1 = (e1 * inv).astype(bf16)
            p2 = (e2 * inv).astype(bf16)
            o = jnp.dot(p1, vi, preferred_element_type=f32) + jnp.dot(p2, vt, preferred_element_type=f32)
            ret[h, :, i] = o.astype(bf16).reshape(NS, depth, HD)

        rb[h, s] = ret[h, 0]

        @pl.loop(1, NS)
        def _(r):
            rcopy(h, r, source(r)).start()

    eye = iota((rows, rows), 0) == iota((rows, rows), 1)

    def to_col(row):
        return jnp.sum(jnp.where(eye, jnp.broadcast_to(row, (rows, rows)), 0.0), axis=1, keepdims=True)

    def to_row(col):
        return jnp.sum(jnp.where(eye, jnp.broadcast_to(col, (rows, rows)), 0.0), axis=0, keepdims=True)

    pick = (jnp.broadcast_to(to_col(pos), (rows, slots)) == iota((rows, slots), 1).astype(f32)).astype(bf16)
    wout_over_cores()
    for h in range(heads):
        copy(rb.at[h, most], rb.at[h, most], rss.at[h], rrs.at[h], seq=sib).wait_recv()
        av[m, h] = jnp.dot(pick, rb[h].reshape(slots, HD), preferred_element_type=f32).astype(bf16)
        for to in (right, left, far):
            acopy(h, to).start()

    wout_in()

    def part(y):
        a = jnp.concatenate([av[y, h] for h in range(heads)], axis=1)
        return jnp.dot(a, wc[y], preferred_element_type=f32)

    acc = part(m)
    for y in (right, left, far):
        copy(av.at[y], av.at[y], y2s.at[0], y2r.at[y], mp=right).wait_recv()
        acc = acc + part(y)

    mean = jnp.sum(acc, axis=1, keepdims=True) / cols
    dev = acc - mean
    m2 = jnp.sum(dev * dev, axis=1, keepdims=True)
    st[0:1, :] = to_row(mean)
    st[1:2, :] = to_row(m2)

    def scopy(k, to):
        return pltpu.make_async_remote_copy(
            src_ref=st, dst_ref=sr.at[k], send_sem=sss.at[k], recv_sem=srs.at[k],
            device_id={"mp": to}, device_id_type=MESH)

    for k in (1, 3, 2):
        scopy(k, lax.rem(m + k, MP)).start()

    copy(mr.at[most], mr.at[most], mss.at[0], mrsem.at[0], seq=sib).wait_send()
    copy(xs.at[most], xs.at[most], zss.at[0], zrs.at[0], seq=sib).wait_send()
    for i in range(2):
        copy(ts.at[i, most], ts.at[i, most], tss.at[i], trs.at[i], seq=sib).wait_send()
    for h in range(heads):
        copy(ret.at[h, most], ret.at[h, most], rss.at[h], rrs.at[h], seq=sib).wait_send()
    drain1()
    copy(av.at[pl.ds(0, MP - 1)], av.at[pl.ds(0, MP - 1)], y2s.at[0], y2r.at[0], mp=right).wait_send()
    wout_drain()

    for k in (1, 3, 2):
        scopy(k, lax.rem(m + k, MP)).wait()

    means = [st[0:1, :]] + [sr[k, 0:1, :] for k in (1, 2, 3)]
    m2s = [st[1:2, :]] + [sr[k, 1:2, :] for k in (1, 2, 3)]
    avg = sum(means) / MP
    sq = sum(m2s) + cols * sum((u - avg) * (u - avg) for u in means)
    rstd = lax.rsqrt(sq / (MP * cols) + EPS)
    avg_c = to_col(avg)
    rstd_c = to_col(rstd)
    own = pl.ds(pl.multiple_of(m * cols, 128), cols)
    n = (acc - avg_c) * rstd_c * qg_ref[:, own] + qb_ref[:, own]
    o_ref[...] = (x_ref[...].astype(f32) + n).astype(bf16)


def shards(
    patches, image_of, prompt_of, text_len, text_kv, w_qkv, w_out, pre_gain, pre_bias, post_gain, post_bias,
):
    NS = lax.axis_size("seq")
    MP = lax.axis_size("mp")
    rows, cols = patches.shape
    depth = rows // NS
    hc = w_out.shape[0]
    toks = text_kv.shape[1]
    heads = hc // HD
    text = text_kv
    w = jnp.transpose(w_qkv, (1, 0, 2))
    full = w_qkv.shape[0]
    vm = pl.BlockSpec(memory_space=pltpu.VMEM)
    sm = pl.BlockSpec(memory_space=pltpu.SMEM)
    anys = pl.BlockSpec(memory_space=pl.ANY)
    dma = pltpu.SemaphoreType.DMA
    return pl.pallas_call(
        fused,
        out_shape=jax.ShapeDtypeStruct((rows, cols), bf16),
        in_specs=[anys, anys, sm, sm, anys, anys, anys, anys, anys, anys, anys],
        out_specs=vm,
        scratch_shapes=[
            pltpu.VMEM((rows, cols), bf16),
            pltpu.VMEM((1, rows), i32),
            pltpu.VMEM((1, full), f32),
            pltpu.VMEM((1, full), f32),
            pltpu.VMEM((1, full), f32),
            pltpu.VMEM((1, full), f32),
            pltpu.VMEM((NS, 2, depth, cols), bf16),
            pltpu.VMEM((MP, NS, 2, depth, cols), bf16),
            pltpu.VMEM((2, 2, NS // 2, depth, full), bf16),
            pltpu.VMEM((3, full, hc), bf16),
            pltpu.VMEM((MP, hc, cols), bf16),
            pltpu.VMEM((3, 2, 2, NS * depth // 2, hc), bf16),
            pltpu.VMEM((2, NS, 2, toks, hc), bf16),
            pltpu.VMEM((2, NS, 2, toks, hc), bf16),
            pltpu.VMEM((heads, NS, 2, depth, HD), bf16),
            pltpu.VMEM((heads, NS, 2, depth, HD), bf16),
            pltpu.VMEM((MP, heads, rows, HD), bf16),
            pltpu.VMEM(text_kv.shape, bf16),
            pltpu.VMEM((1, 128), i32),
            pltpu.VMEM((NS, 1, 128), i32),
            pltpu.SMEM((NS, 1, 128), i32),
            pltpu.VMEM((8, rows), f32),
            pltpu.VMEM((MP, 8, rows), f32),
            pltpu.VMEM((4, 1, NS * depth), f32),
            dma((1,)), dma((NS,)), dma((2,)), dma((2,)), dma((1,)), dma((1,)),
            dma((4,)), dma((4, NS)), dma((heads,)), dma((heads,)), dma((1,)), dma((MP,)),
            dma((MP,)), dma((MP,)), dma((MP,)), dma((MP,)), dma((MP,)), dma((MP,)),
            dma((10,)),
        ],
        compiler_params=pltpu.CompilerParams(collective_id=0, has_side_effects=True, vmem_limit_bytes=58 << 20),
    )(
        patches, image_of.reshape(1, rows), prompt_of, text_len, text, w, w_out,
        pre_gain.reshape(1, -1), pre_bias.reshape(1, -1), post_gain.reshape(1, -1), post_bias.reshape(1, -1),
    )


def solution(mesh):
    placed = (
        P(("dp", "seq"), "mp"),
        P(("dp", "seq")),
        P("dp", "seq"),
        P("dp", None),
        P("dp", "seq", None, "mp"),
        P(None, None, "mp"),
        P("mp", None),
        P(),
        P(),
        P(),
        P(),
    )
    return jax.shard_map(
        shards, mesh=mesh, in_specs=placed, out_specs=P(("dp", "seq"), "mp"), check_vma=False
    )
```

```python
import math

import jax
import jax.numpy as jnp
from jax import lax
from jax.experimental import pallas as pl
from jax.experimental.pallas import tpu as pltpu
from jax.sharding import PartitionSpec as P

HD = 128
EPS = 1e-05
MESH = pl.DeviceIdType.MESH
NEG = -1e30

f32 = jnp.float32
bf16 = jnp.bfloat16
i32 = jnp.int32


def iota(shape, dim):
    return lax.broadcasted_iota(i32, shape, dim)


def fused(
    x_in, img_in, prm_ref, len_ref, text_ref, w_ref, wo_ref, pg_in, pb_in, qg_in, qb_in,
    o_ref,
    x_ref, img_ref, pg_ref, pb_ref, qg_ref, qb_ref, xs, xg, xn, wv, wc, qkv, ts, tr, ret, rb, av, tx, ms, mr, mrs, st, sr, kb,
    zss, zrs, tss, trs, mss, mrsem, yss, yrs, rss, rrs, y2s, y2r, wss, wrs, bss, brs, sss, srs, lsem,
):
    s = lax.axis_index("seq")
    m = lax.axis_index("mp")
    NS, MP = xg.shape[1], xg.shape[0]
    rows = x_ref.shape[0]
    cols = x_ref.shape[1]
    slots = xs.shape[2] * xs.shape[1] * NS
    depth = xs.shape[2]
    nimg = 2 * NS
    heads = qkv.shape[-1] // HD
    right = lax.rem(m + 1, MP)
    left = lax.rem(m + MP - 1, MP)
    far = lax.rem(m + 2, MP)
    core = lax.rem(s, 2)
    sib = s + 1 - 2 * core

    NP = NS // 2
    pair = s // 2

    def seq_at(k):
        return lax.rem(s + k, NS)

    def hop(v):
        far_by = (v + 1) // 2
        return jnp.where(lax.rem(v, 2) == 1, far_by, NP - far_by)

    def to_pair(v):
        return lax.rem(pair + hop(v), NP)

    def from_pair(v):
        return lax.rem(pair + 2 * NP - hop(v), NP)

    def source(r):
        return 2 * from_pair(r // 2) + lax.rem(r + core, 2)

    bar = pltpu.get_barrier_semaphore()

    @pl.loop(1, NS)
    def _(k):
        pl.semaphore_signal(bar, inc=1, device_id={"seq": seq_at(k)}, device_id_type=MESH)

    for d in (right, left, far):
        pl.semaphore_signal(bar, inc=1, device_id={"mp": d}, device_id_type=MESH)

    loads = []
    for n, (a, b) in enumerate(
        ((img_in, img_ref), (x_in, x_ref), (pg_in, pg_ref), (pb_in, pb_ref), (qg_in, qg_ref), (qb_in, qb_ref), (text_ref, tx))
    ):
        loads.append(pltpu.make_async_copy(a, b, lsem.at[3 + n]))
        loads[-1].start()
    wcp = pltpu.make_async_copy(w_ref, wv, lsem.at[0])
    wcp.start()
    ocp = pltpu.make_async_copy(wo_ref.at[:, pl.ds(pl.multiple_of(m * cols, 128), cols)], wc.at[m], lsem.at[1])
    ocp.start()

    loads[0].wait()
    img = img_ref[...]
    onehot = (jnp.broadcast_to(img, (nimg, rows)) == iota((nimg, rows), 0)).astype(f32)
    upto = (iota((rows, rows), 0) <= iota((rows, rows), 1)).astype(bf16)
    cum = jnp.dot(onehot.astype(bf16), upto, preferred_element_type=f32)
    rank = jnp.sum(cum * onehot, axis=0, keepdims=True) - 1.0
    pos = img.astype(f32) * depth + rank
    counts = jnp.sum(onehot, axis=1, keepdims=True)
    crow = jnp.sum(
        jnp.where(iota((nimg, 128), 0) == iota((nimg, 128), 1), jnp.broadcast_to(counts, (nimg, 128)), 0.0),
        axis=0, keepdims=True,
    ).astype(i32)
    lane = iota((1, 128), 1)
    crow = jnp.where(lane == nimg, prm_ref[0, 0], jnp.where(lane == nimg + 1, prm_ref[0, 1], crow))
    ms[...] = crow
    mr[s] = crow
    place = (jnp.broadcast_to(pos, (slots, rows)) == iota((slots, rows), 0).astype(f32)).astype(bf16)
    loads[1].wait()
    spread = jnp.dot(place, x_ref[...], preferred_element_type=f32).astype(bf16)
    xs[...] = spread.reshape(xs.shape)
    xg[m, s] = xs[s]

    pl.semaphore_wait(bar, NS - 1 + MP - 1)

    def copy(src, dst, ss, rs, **to):
        return pltpu.make_async_remote_copy(
            src_ref=src, dst_ref=dst, send_sem=ss, recv_sem=rs, device_id=to, device_id_type=MESH)

    def zcopy(d):
        return copy(xs.at[d], xg.at[m, s], zss.at[0], zrs.at[s], seq=d)

    def zgot(c):
        copy(xg.at[m, c], xg.at[m, c], zss.at[0], zrs.at[c], seq=sib).wait_recv()

    def tcopy(i, d):
        return copy(ts.at[i, d], tr.at[i, s], tss.at[i], trs.at[i], seq=d)

    def mcopy(d):
        return copy(ms, mr.at[s], mss.at[0], mrsem.at[0], seq=d)

    def rcopy(h, r, d):
        return copy(ret.at[h, r], rb.at[h, s], rss.at[h], rrs.at[h], seq=d)

    def acopy(h, to):
        return copy(av.at[m, h], av.at[m, h], y2s.at[0], y2r.at[m], mp=to)

    most = pl.ds(0, NS - 1)

    def each_other(start):
        @pl.loop(1, NS)
        def _(r):
            start(2 * to_pair(r // 2) + lax.rem(r + core, 2)).start()

    def unit1(y, c, n, to):
        ref = xg.at[y, c] if n < 2 else xg.at[y, c, n - 2]
        return copy(ref, ref, yss.at[n], yrs.at[n, c], mp=to)

    def open1(j):
        unit1(m, j, 0, right).start()
        unit1(m, j, 1, left).start()

    def pass1(j):
        unit1(left, j, 0, right).wait_recv()
        unit1(left, j, 2, right).start()
        unit1(right, j, 1, left).wait_recv()
        unit1(right, j, 3, left).start()

    def arrived1(j):
        unit1(far, j, 2, right).wait_recv()
        unit1(far, j, 3, left).wait_recv()

    def drain1():
        for n in range(4):
            ref = xg.at[m] if n < 2 else xg.at[m, pl.ds(0, NP)]
            copy(ref, ref, yss.at[n], yrs.at[n, 0], mp=right).wait_send()

    hrows = wc.shape[1] // 2

    def half(co):
        return pl.ds(pl.multiple_of(co * hrows, 16), hrows)

    def wcopy(to, y, k):
        return pltpu.make_async_remote_copy(
            src_ref=wo_ref.at[half(core), pl.ds(pl.multiple_of(to * cols, 128), cols)], dst_ref=wc.at[y, half(core)],
            send_sem=wss.at[k], recv_sem=wrs.at[k], device_id={"mp": to}, device_id_type=MESH)

    def bcopy(y, k, part):
        return pltpu.make_async_remote_copy(
            src_ref=wc.at[y, part], dst_ref=wc.at[y, part], send_sem=bss.at[k], recv_sem=brs.at[k],
            device_id={"seq": sib}, device_id_type=MESH)

    YS = [(k, lax.rem(m + k, MP), lax.rem(m + MP - k, MP)) for k in (1, 3, 2)]

    def wout_out():
        for k, to, _ in YS:
            wcopy(to, m, k).start()

    def wout_over_cores():
        for k, _, y in YS:
            wcopy(y, y, k).wait_recv()
            bcopy(y, k, half(core)).start()

    def wout_in():
        ocp.wait()
        for k, _, y in YS:
            bcopy(y, k, half(1 - core)).wait_recv()

    def wout_drain():
        for k, to, y in YS:
            wcopy(to, m, k).wait_send()
            bcopy(y, k, half(core)).wait_send()

    open1(s)
    each_other(mcopy)
    each_other(zcopy)

    LAG1 = 6
    LAG2 = 12
    TM = 6
    T0 = 8
    T1 = 14

    def text_out():
        loads[6].wait()
        copy(mr.at[most], mr.at[most], mss.at[0], mrsem.at[0], seq=sib).wait_recv()
        scp = pltpu.make_async_copy(mr, mrs, lsem.at[2])
        scp.start()
        scp.wait()

        @pl.loop(0, NS)
        def _(d):
            for i in range(2):
                both = tx[mrs[d, 0, nimg + i]]
                ts[i, d, 0] = both[:, 0, :]
                ts[i, d, 1] = both[:, 1, :]

        for i in range(2):
            tr[i, s] = ts[i, s]

        for n in range(2, 6):
            loads[n].wait()
        wcp.wait()

    def project(hf, j):
        r = jnp.dot(xn[hf].reshape(slots // 2, MP * cols), wv[j], preferred_element_type=f32).astype(bf16)
        qkv[j, :, hf] = r.reshape(2, slots // 4, r.shape[-1])

    def norm_chunk(c, hf, r):
        parts = [xg[y, c].astype(f32) for y in range(MP)]
        total = sum(jnp.sum(p, axis=-1, keepdims=True) for p in parts)
        mean = total / (MP * cols)
        parts = [p - mean for p in parts]
        var = sum(jnp.sum(p * p, axis=-1, keepdims=True) for p in parts) / (MP * cols)
        inv = lax.rsqrt(var + EPS)
        for y in range(MP):
            g = pg_ref[:, y * cols:(y + 1) * cols].reshape(1, 1, cols)
            b = pb_ref[:, y * cols:(y + 1) * cols].reshape(1, 1, cols)
            n = (parts[y] * inv * g + b).astype(bf16)
            for i in range(2):
                xn[hf, i, r, :, y * cols:(y + 1) * cols] = n[i]

    @pl.loop(0, NS + LAG2)
    def _(t):
        @pl.when((t > 0) & (t < NS))
        def _():
            zgot(source(t))

        @pl.when((t > 0) & (t < NS))
        def _():
            open1(source(t))

        @pl.when(t == TM)
        def _():
            text_out()

        @pl.when(t == T0)
        def _():
            each_other(lambda d: tcopy(0, d))

        @pl.when(t == T1)
        def _():
            each_other(lambda d: tcopy(1, d))

        @pl.when((t >= LAG1) & (t < NS + LAG1))
        def _():
            pass1(source(t - LAG1))

        @pl.when(t == NS + LAG1)
        def _():
            wout_out()

        @pl.when(t >= LAG2)
        def _():
            c = source(t - LAG2)
            arrived1(c)
            norm_chunk(c, (t - LAG2) // NP, lax.rem(t - LAG2, NP))

        @pl.when((t >= LAG2 + NP - 1) & (t < LAG2 + NP + 2))
        def _():
            project(0, t - (LAG2 + NP - 1))

    @pl.loop(0, 3)
    def _(j):
        project(1, j)

    span = NS * depth
    lanes = iota((1, span), 1)
    tlen = NS * depth
    for i in range(2):
        cnt = jnp.zeros((1, span), i32)
        for r in range(NS):
            cnt = jnp.where(lanes // depth == r, mrs[source(r), 0, 2 * s + i], cnt)
        kb[2 * i] = jnp.where(lax.rem(lanes, depth) < cnt, 0.0, NEG)
        n = len_ref[0, mrs[s, 0, nimg + i]]
        kb[2 * i + 1] = jnp.where(lanes < n, 0.0, NEG)

    scale = 1.0 / math.sqrt(HD)
    nt = (((1,), (1,)), ((), ()))
    for i in range(2):
        copy(tr.at[i, most], tr.at[i, most], tss.at[i], trs.at[i], seq=sib).wait_recv()

    for h in range(heads):
        hs = slice(h * HD, (h + 1) * HD)

        @pl.loop(0, 2)
        def _(i):
            bi = kb[2 * i]
            bt = kb[2 * i + 1]
            q, ki, vi = (qkv[n, i, :, :, hs].reshape(tlen, HD) for n in range(3))
            kt = tr[i, :, 0, :, hs].reshape(tlen, HD)
            vt = tr[i, :, 1, :, hs].reshape(tlen, HD)
            s1 = lax.dot_general(q, ki, nt, preferred_element_type=f32) * scale + bi
            s2 = lax.dot_general(q, kt, nt, preferred_element_type=f32) * scale + bt
            top = jnp.maximum(jnp.max(s1, axis=-1, keepdims=True), jnp.max(s2, axis=-1, keepdims=True))
            e1 = jnp.exp(s1 - top)
            e2 = jnp.exp(s2 - top)
            tot = jnp.sum(e1, axis=-1, keepdims=True) + jnp.sum(e2, axis=-1, keepdims=True)
            inv = 1.0 / tot
            p1 = (e1 * inv).astype(bf16)
            p2 = (e2 * inv).astype(bf16)
            o = jnp.dot(p1, vi, preferred_element_type=f32) + jnp.dot(p2, vt, preferred_element_type=f32)
            ret[h, :, i] = o.astype(bf16).reshape(NS, depth, HD)

        rb[h, s] = ret[h, 0]

        @pl.loop(1, NS)
        def _(r):
            rcopy(h, r, source(r)).start()

    eye = iota((rows, rows), 0) == iota((rows, rows), 1)

    def to_col(row):
        return jnp.sum(jnp.where(eye, jnp.broadcast_to(row, (rows, rows)), 0.0), axis=1, keepdims=True)

    def to_row(col):
        return jnp.sum(jnp.where(eye, jnp.broadcast_to(col, (rows, rows)), 0.0), axis=0, keepdims=True)

    pick = (jnp.broadcast_to(to_col(pos), (rows, slots)) == iota((rows, slots), 1).astype(f32)).astype(bf16)
    wout_over_cores()
    for h in range(heads):
        copy(rb.at[h, most], rb.at[h, most], rss.at[h], rrs.at[h], seq=sib).wait_recv()
        av[m, h] = jnp.dot(pick, rb[h].reshape(slots, HD), preferred_element_type=f32).astype(bf16)
        for to in (right, left, far):
            acopy(h, to).start()

    wout_in()

    def part(y):
        a = jnp.concatenate([av[y, h] for h in range(heads)], axis=1)
        return jnp.dot(a, wc[y], preferred_element_type=f32)

    acc = part(m)
    for y in (right, left, far):
        copy(av.at[y], av.at[y], y2s.at[0], y2r.at[y], mp=right).wait_recv()
        acc = acc + part(y)

    mean = jnp.sum(acc, axis=1, keepdims=True) / cols
    dev = acc - mean
    m2 = jnp.sum(dev * dev, axis=1, keepdims=True)
    st[0:1, :] = to_row(mean)
    st[1:2, :] = to_row(m2)

    def scopy(k, to):
        return pltpu.make_async_remote_copy(
            src_ref=st, dst_ref=sr.at[k], send_sem=sss.at[k], recv_sem=srs.at[k],
            device_id={"mp": to}, device_id_type=MESH)

    for k in (1, 3, 2):
        scopy(k, lax.rem(m + k, MP)).start()

    copy(mr.at[most], mr.at[most], mss.at[0], mrsem.at[0], seq=sib).wait_send()
    copy(xs.at[most], xs.at[most], zss.at[0], zrs.at[0], seq=sib).wait_send()
    for i in range(2):
        copy(ts.at[i, most], ts.at[i, most], tss.at[i], trs.at[i], seq=sib).wait_send()
    for h in range(heads):
        copy(ret.at[h, most], ret.at[h, most], rss.at[h], rrs.at[h], seq=sib).wait_send()
    drain1()
    copy(av.at[pl.ds(0, MP - 1)], av.at[pl.ds(0, MP - 1)], y2s.at[0], y2r.at[0], mp=right).wait_send()
    wout_drain()

    for k in (1, 3, 2):
        scopy(k, lax.rem(m + k, MP)).wait()

    means = [st[0:1, :]] + [sr[k, 0:1, :] for k in (1, 2, 3)]
    m2s = [st[1:2, :]] + [sr[k, 1:2, :] for k in (1, 2, 3)]
    avg = sum(means) / MP
    sq = sum(m2s) + cols * sum((u - avg) * (u - avg) for u in means)
    rstd = lax.rsqrt(sq / (MP * cols) + EPS)
    avg_c = to_col(avg)
    rstd_c = to_col(rstd)
    own = pl.ds(pl.multiple_of(m * cols, 128), cols)
    n = (acc - avg_c) * rstd_c * qg_ref[:, own] + qb_ref[:, own]
    o_ref[...] = (x_ref[...].astype(f32) + n).astype(bf16)


def shards(
    patches, image_of, prompt_of, text_len, text_kv, w_qkv, w_out, pre_gain, pre_bias, post_gain, post_bias,
):
    NS = lax.axis_size("seq")
    MP = lax.axis_size("mp")
    rows, cols = patches.shape
    depth = rows // NS
    hc = w_out.shape[0]
    toks = text_kv.shape[1]
    heads = hc // HD
    text = text_kv
    w = jnp.transpose(w_qkv, (1, 0, 2))
    full = w_qkv.shape[0]
    vm = pl.BlockSpec(memory_space=pltpu.VMEM)
    sm = pl.BlockSpec(memory_space=pltpu.SMEM)
    anys = pl.BlockSpec(memory_space=pl.ANY)
    dma = pltpu.SemaphoreType.DMA
    return pl.pallas_call(
        fused,
        out_shape=jax.ShapeDtypeStruct((rows, cols), bf16),
        in_specs=[anys, anys, sm, sm, anys, anys, anys, anys, anys, anys, anys],
        out_specs=vm,
        scratch_shapes=[
            pltpu.VMEM((rows, cols), bf16),
            pltpu.VMEM((1, rows), i32),
            pltpu.VMEM((1, full), f32),
            pltpu.VMEM((1, full), f32),
            pltpu.VMEM((1, full), f32),
            pltpu.VMEM((1, full), f32),
            pltpu.VMEM((NS, 2, depth, cols), bf16),
            pltpu.VMEM((MP, NS, 2, depth, cols), bf16),
            pltpu.VMEM((2, 2, NS // 2, depth, full), bf16),
            pltpu.VMEM((3, full, hc), bf16),
            pltpu.VMEM((MP, hc, cols), bf16),
            pltpu.VMEM((3, 2, 2, NS * depth // 2, hc), bf16),
            pltpu.VMEM((2, NS, 2, toks, hc), bf16),
            pltpu.VMEM((2, NS, 2, toks, hc), bf16),
            pltpu.VMEM((heads, NS, 2, depth, HD), bf16),
            pltpu.VMEM((heads, NS, 2, depth, HD), bf16),
            pltpu.VMEM((MP, heads, rows, HD), bf16),
            pltpu.VMEM(text_kv.shape, bf16),
            pltpu.VMEM((1, 128), i32),
            pltpu.VMEM((NS, 1, 128), i32),
            pltpu.SMEM((NS, 1, 128), i32),
            pltpu.VMEM((8, rows), f32),
            pltpu.VMEM((MP, 8, rows), f32),
            pltpu.VMEM((4, 1, NS * depth), f32),
            dma((1,)), dma((NS,)), dma((2,)), dma((2,)), dma((1,)), dma((1,)),
            dma((4,)), dma((4, NS)), dma((heads,)), dma((heads,)), dma((1,)), dma((MP,)),
            dma((MP,)), dma((MP,)), dma((MP,)), dma((MP,)), dma((MP,)), dma((MP,)),
            dma((10,)),
        ],
        compiler_params=pltpu.CompilerParams(collective_id=0, has_side_effects=True, vmem_limit_bytes=58 << 20),
    )(
        patches, image_of.reshape(1, rows), prompt_of, text_len, text, w, w_out,
        pre_gain.reshape(1, -1), pre_bias.reshape(1, -1), post_gain.reshape(1, -1), post_bias.reshape(1, -1),
    )


def solution(mesh):
    placed = (
        P(("dp", "seq"), "mp"),
        P(("dp", "seq")),
        P("dp", "seq"),
        P("dp", None),
        P("dp", "seq", None, "mp"),
        P(None, None, "mp"),
        P("mp", None),
        P(),
        P(),
        P(),
        P(),
    )
    return jax.shard_map(
        shards, mesh=mesh, in_specs=placed, out_specs=P(("dp", "seq"), "mp"), check_vma=False
    )
```
